128 devices in a mesh: gx: 8 (over y, core), gy: 16 (over z, x).
Axes of the slice: x: 4, y: 4, z: 4, core: 2. Of those that a mesh axis runs over, the one named last changes fastest.
Arguments:
- adjoint_state: float32 [9, 8, 512, 1024], P(None, None, 'gy', 'gx'), may hold values from -6 to 6
- lame_lambda: float32 [8, 512, 1024], P(None, 'gy', 'gx'), may hold values from 0.5 to 1.5
- shear_modulus: float32 [8, 512, 1024], P(None, 'gy', 'gx'), may hold values from 0.3 to 0.9
- buoyancy: float32 [8, 512, 1024], P(None, 'gy', 'gx'), may hold values from 0.6 to 1.2
- forward_dilation: bfloat16 [8, 8, 512, 1024], P(None, None, 'gy', 'gx'), may hold values from -6 to 6
- forward_shear: bfloat16 [8, 8, 512, 1024], P(None, None, 'gy', 'gx'), may hold values from -6 to 6
- residual: bfloat16 [12288, 3, 4096], P(('gx', 'gy')), may hold values from -6 to 6
- sample_counts: int32 [12288], P(('gx', 'gy')), may hold values from 2048 to 4096
- station_list: int32 [12288], P(('gx', 'gy')), may hold values from 0 to 511, as said below
- receiver_cells: int32 [512], P(('gx', 'gy')), may hold values from 0 to 524287, as said below
- tile_map: int32 [32768], P(('gx', 'gy')), may hold values from 0 to 32767, as said below
Outputs:
- model_kernels: float32 [2, 8, 32768], P(None, None, ('gx', 'gy'))
- adjoint_out: float32 [9, 8, 512, 1024], P(None, None, 'gy', 'gx')
The draws below stay inside these ranges and needn't reach their ends.
Inputs may be any that keep to these rules, and one draw needn't show every extreme that they name: `station_list`: station s belongs to the device of index s // 4 (the order of the joined axes gx, gy). The rows of one device name stations of any one owner at most 2 times; in every draw some owner is named exactly 2 times by the rows of every device. `receiver_cells`: station s's cell lies in the tile of the device of index s // 4, on the surface; the first station sits at the grid's first corner and the last station at its last corner. `tile_map`: A permutation. The 256 columns of device p go 2 to each device q, into the slots q * 256 + p * 2 to q * 256 + (p + 1) * 2 - 1.
All inputs are finite; a program needn't handle non-finite values.
Results may differ from the reference program's by a relative error of at most 0.0003.
Values may be sent and summed in bfloat16 or wider, within the bound.
No kernel may reach another device: no remote copies, remote signals or barrier semaphores. Data moves between devices by JAX's collectives and lax.ppermute only.
A program may use at most 128 MiB of HBM per device.

```python
import math
import jax
import jax.numpy as jnp

CX = 128
CY = 32
NZ = 8
STEPS = 8
SAMPLES = 4096
ROWS_DEV = 96
STA_DEV = 4
OWNERS = 128
CAP = 2
NX = 1024
NY = 512
ROWS = 12288
STATIONS = 512
COLS_DEV = 256
COLS = 32768
PER = 2
N_GX = 8
N_GY = 16


def draw_station_list(key, part):
    busy_owner = jax.random.randint(jax.random.fold_in(key, 11), (), 0, OWNERS)

    def block_draw(block_index):
        block_key = jax.random.fold_in(jax.random.fold_in(key, 12), block_index)
        shuffled = jax.random.permutation(jax.random.fold_in(block_key, 1), CAP * (OWNERS - 1))[:ROWS_DEV - CAP] // CAP
        others = (shuffled + (shuffled >= busy_owner).astype(jnp.int32)).astype(jnp.int32)
        owner_dev = jnp.concatenate([jnp.full((CAP,), busy_owner, jnp.int32), others])
        row_order = jax.random.permutation(jax.random.fold_in(block_key, 2), ROWS_DEV)
        local_pick = jax.random.randint(jax.random.fold_in(block_key, 3), (ROWS_DEV,), 0, STA_DEV)
        return owner_dev[row_order] * STA_DEV + local_pick
    return jax.vmap(block_draw)(jnp.arange(OWNERS)).reshape(ROWS).astype(jnp.int32)


def draw_receiver_cells(key, part):
    station = jnp.arange(STATIONS)
    device = station // STA_DEV
    tile_x = device // (NY // CY)
    tile_y = device % (NY // CY)
    column = tile_x * CX + jax.random.randint(jax.random.fold_in(key, 21), (STATIONS,), 0, CX)
    row_pick = tile_y * CY + jax.random.randint(jax.random.fold_in(key, 22), (STATIONS,), 0, CY)
    column = column.at[0].set(0).at[STATIONS - 1].set(NX - 1)
    row_pick = row_pick.at[0].set(0).at[STATIONS - 1].set(NY - 1)
    return (row_pick * NX + column).astype(jnp.int32)


def draw_tile_map(key, part):

    def device_draw(device):
        shuffled = jax.random.permutation(jax.random.fold_in(jax.random.fold_in(key, 31), device), COLS_DEV)
        target = shuffled // PER
        within = shuffled % PER
        return target * COLS_DEV + device * PER + within
    return jax.vmap(device_draw)(jnp.arange(OWNERS)).reshape(COLS).astype(jnp.int32)


def plant(values, stream_key, least, top_value):
    extent = values.shape
    index_at = [jax.random.randint(jax.random.fold_in(stream_key, axis), (), 0, extent[axis]) for axis in range(len(extent))]
    values = values.at[tuple(index_at)].set(least)
    longest = extent.index(max(extent))
    index_at[longest] = (index_at[longest] + 1) % extent[longest]
    return values.at[tuple(index_at)].set(top_value)


def shard_levels(stream_key, shape, shards, smallest, high):
    level = 1.0
    for dim, parts in shards:
        steps = jax.random.uniform(jax.random.fold_in(jax.random.fold_in(stream_key, 6), dim), (parts,), jnp.float32, smallest / len(shards), high / len(shards))
        level = level * jnp.repeat(jnp.exp(steps), shape[dim] // parts).reshape((-1,) + (1,) * (len(shape) - 1 - dim))
    return level


def centred(rng, shape, scale, reach, shards=(), held_as=jnp.bfloat16):
    level = shard_levels(rng, shape, shards, -0.22, 0.18) if shards else 1.0
    array = jax.random.normal(rng, shape, jnp.float32) * scale * level
    return jnp.minimum(jnp.maximum(array, -reach), reach).astype(held_as)


def setup_inputs(seed: int = 0) -> dict:
    arg_keys = jax.random.split(jax.random.key(seed), 12)
    adjoint_state = centred(arg_keys[0], (9, NZ, NY, NX), 1.0, 6.0, ((2, 16), (3, 8)), jnp.float32)
    lame_lambda = jnp.clip(0.5 + 1.0 * jax.random.uniform(arg_keys[1], (NZ, NY, NX), jnp.float32) ** shard_levels(arg_keys[1], (NZ, NY, NX), ((1, 16), (2, 8)), -0.2, 0.2), 0.5, 1.5)
    shear_modulus = jnp.clip(0.3 + 0.59999996 * jax.random.uniform(arg_keys[2], (NZ, NY, NX), jnp.float32) ** shard_levels(arg_keys[2], (NZ, NY, NX), ((1, 16), (2, 8)), -0.2, 0.2), 0.3, 0.9)
    buoyancy = jnp.clip(0.6 + 0.6 * jax.random.uniform(arg_keys[3], (NZ, NY, NX), jnp.float32) ** shard_levels(arg_keys[3], (NZ, NY, NX), ((1, 16), (2, 8)), -0.2, 0.2), 0.6, 1.2)
    forward_dilation = centred(arg_keys[4], (STEPS, NZ, NY, NX), 1.0, 6.0, ((2, 16), (3, 8)))
    forward_shear = centred(arg_keys[5], (STEPS, NZ, NY, NX), 1.0, 6.0, ((2, 16), (3, 8)))
    residual = centred(arg_keys[6], (ROWS, 3, SAMPLES), 1.0, 6.0, ((0, 128),))
    sample_counts = plant(jax.random.randint(arg_keys[7], (ROWS,), SAMPLES // 2, SAMPLES + 1), jax.random.fold_in(arg_keys[7], 1), SAMPLES // 2, SAMPLES).astype(jnp.int32)
    station_list = draw_station_list(jax.random.fold_in(arg_keys[11], 71), 0)
    receiver_cells = draw_receiver_cells(jax.random.fold_in(arg_keys[11], 71), 0)
    tile_map = draw_tile_map(jax.random.fold_in(arg_keys[11], 71), 0)
    return {"adjoint_state": adjoint_state, "lame_lambda": lame_lambda, "shear_modulus": shear_modulus, "buoyancy": buoyancy, "forward_dilation": forward_dilation, "forward_shear": forward_shear, "residual": residual, "sample_counts": sample_counts, "station_list": station_list, "receiver_cells": receiver_cells, "tile_map": tile_map}


time_step = 0.25

def ahead_x(padded):
    return padded[1:-1, 1:-1, 2:] - padded[1:-1, 1:-1, 1:-1]

def behind_x(padded):
    return padded[1:-1, 1:-1, 1:-1] - padded[1:-1, 1:-1, :-2]

def ahead_y(padded):
    return padded[1:-1, 2:, 1:-1] - padded[1:-1, 1:-1, 1:-1]

def behind_y(padded):
    return padded[1:-1, 1:-1, 1:-1] - padded[1:-1, :-2, 1:-1]

def ahead_z(padded):
    return padded[2:, 1:-1, 1:-1] - padded[1:-1, 1:-1, 1:-1]

def behind_z(padded):
    return padded[1:-1, 1:-1, 1:-1] - padded[:-2, 1:-1, 1:-1]

def velocity_update(velocity, stress_pad, buoyancy, source_now):
    accel_x = ahead_x(stress_pad[0]) + behind_y(stress_pad[3]) + behind_z(stress_pad[4])
    accel_y = behind_x(stress_pad[3]) + ahead_y(stress_pad[1]) + behind_z(stress_pad[5])
    accel_z = behind_x(stress_pad[4]) + behind_y(stress_pad[5]) + ahead_z(stress_pad[2])
    velocity = velocity + time_step * buoyancy * jnp.stack([accel_x, accel_y, accel_z])
    return velocity.at[:, 0].add(time_step * buoyancy[0] * source_now)

def stress_update(stress, vel_pad, lame_lambda, shear_modulus):
    strain_xx = behind_x(vel_pad[0])
    strain_yy = behind_y(vel_pad[1])
    strain_zz = behind_z(vel_pad[2])
    dilation = strain_xx + strain_yy + strain_zz
    strain_xy = ahead_y(vel_pad[0]) + ahead_x(vel_pad[1])
    strain_xz = ahead_z(vel_pad[0]) + ahead_x(vel_pad[2])
    strain_yz = ahead_z(vel_pad[1]) + ahead_y(vel_pad[2])
    pressure = lame_lambda * dilation
    updated = jnp.stack([stress[0] + time_step * (pressure + 2.0 * shear_modulus * strain_xx), stress[1] + time_step * (pressure + 2.0 * shear_modulus * strain_yy), stress[2] + time_step * (pressure + 2.0 * shear_modulus * strain_zz), stress[3] + time_step * shear_modulus * strain_xy, stress[4] + time_step * shear_modulus * strain_xz, stress[5] + time_step * shear_modulus * strain_yz])
    return (updated, dilation, strain_xy)

def resample_table(samples):
    per_step = samples // STEPS
    position = jnp.arange(samples, dtype=jnp.float32) + 0.5
    centers = (jnp.arange(STEPS, dtype=jnp.float32) + 0.5) * per_step
    weight = jnp.maximum(0.0, 1.0 - jnp.abs(position[:, None] - centers[None, :]) / per_step)
    return (weight / math.sqrt(per_step)).astype(jnp.bfloat16)

def reference(adjoint_state, lame_lambda, shear_modulus, buoyancy, forward_dilation, forward_shear, residual, sample_counts, station_list, receiver_cells, tile_map):
    live_mask = jnp.arange(SAMPLES)[None, :] < sample_counts[:, None]
    masked = residual * live_mask[:, None, :].astype(jnp.bfloat16)
    table = resample_table(SAMPLES)
    sources = jnp.dot(masked.reshape(ROWS * 3, SAMPLES), table, preferred_element_type=jnp.float32)
    sources = sources.reshape(ROWS, 3 * STEPS)
    cell_index = receiver_cells[station_list]
    source_plane = jnp.zeros((3 * STEPS, NY * NX), jnp.float32).at[:, cell_index].add(sources.T)
    source_plane = source_plane.reshape(3, STEPS, NY, NX)
    velocity = adjoint_state[0:3]
    stress = adjoint_state[3:9]
    kern_lambda = jnp.zeros((NZ, NY, NX), jnp.float32)
    kern_shear = jnp.zeros((NZ, NY, NX), jnp.float32)
    for instant in range(STEPS):
        stress_pad = jnp.pad(stress, ((0, 0), (1, 1), (1, 1), (1, 1)))
        velocity = velocity_update(velocity, stress_pad, buoyancy, source_plane[:, instant])
        vel_pad = jnp.pad(velocity, ((0, 0), (1, 1), (1, 1), (1, 1)))
        stress, dilation, strain_xy = stress_update(stress, vel_pad, lame_lambda, shear_modulus)
        kern_lambda = kern_lambda + time_step * forward_dilation[instant].astype(jnp.float32) * dilation
        kern_shear = kern_shear + time_step * forward_shear[instant].astype(jnp.float32) * strain_xy
    kernels = jnp.stack([kern_lambda, kern_shear])
    coarse = kernels.reshape(2, NZ, NY // 4, 4, NX // 4, 4).sum(axis=(3, 5)) / 16.0
    coarse = coarse.reshape(2, NZ, N_GY, CY // 4, N_GX, CX // 4).transpose(0, 1, 4, 2, 3, 5).reshape(2, NZ, COLS)
    model_kernels = jnp.zeros((2, NZ, COLS), jnp.float32).at[:, :, tile_map].set(coarse)
    adjoint_out = jnp.concatenate([velocity, stress], 0)
    return (model_kernels, adjoint_out)
```

```python
import math

import jax
import jax.numpy as jnp
import numpy as np
from jax import lax
from jax.experimental import pallas as pl
from jax.experimental.pallas import tpu as pltpu
from jax.sharding import PartitionSpec as P

F32 = jnp.float32
BF16 = jnp.bfloat16

NZ, CY, CX = 8, 32, 128
STEPS = 8
SAMPLES = 4096
H = 0.25
N_GX, N_GY = 8, 16
OWNERS = N_GX * N_GY
NX = N_GX * CX
HALO = 8
ROWS = CY + 2 * HALO
PAD = 8
GROUPS = ROWS // 8
FIELDS = 12
WAVES = 9
PLANES = FIELDS * NZ
EDGES = FIELDS // 2 * GROUPS

AROUND = [(dx, dy) for dx in (-1, 0, 1) for dy in (-1, 0, 1) if (dx, dy) != (0, 0)]

VX, VY, VZ, SXX, SYY, SZZ, SXY, SXZ, SYZ = range(WAVES)

VMEM = pl.BlockSpec(memory_space=pltpu.VMEM)
SMEM = pl.BlockSpec(memory_space=pltpu.SMEM)
ANY = pl.BlockSpec(memory_space=pltpu.HBM)


FULL = pltpu.CompilerParams(vmem_limit_bytes=(64 << 20) - (512 << 10))


def lanes_of(shape):
    return lax.broadcasted_iota(jnp.int32, shape, len(shape) - 1)


def rows_of(shape):
    return lax.broadcasted_iota(jnp.int32, shape, len(shape) - 2)


def roll(value, shift):
    return pltpu.roll(value, shift % value.shape[-1], value.ndim - 1)


def three_parts(value):
    high = value.astype(BF16)
    rest = value - high.astype(F32)
    middle = rest.astype(BF16)
    low = (rest - middle.astype(F32)).astype(BF16)
    return high, middle, low


def resample_table():
    per_step = SAMPLES // STEPS
    position = np.arange(SAMPLES, dtype=np.float32) + np.float32(0.5)
    centers = (np.arange(STEPS, dtype=np.float32) + np.float32(0.5)) * np.float32(per_step)
    distance = np.abs(position[:, None] - centers[None, :]) / np.float32(per_step)
    weight = np.maximum(np.float32(0.0), np.float32(1.0) - distance)
    table = (weight / np.float32(math.sqrt(per_step))).astype(BF16)
    wide = np.zeros((SAMPLES, 128), BF16)
    wide[:, :96] = np.tile(table, (1, 12))
    return wide


def rows_kernel(state, lame, shear, buoyancy, cells, up, down, sems):
    copies = []

    def copy(src, dst):
        made = pltpu.make_async_copy(src, dst, sems.at[len(copies)])
        made.start()
        copies.append(made)

    for to, at in ((up, CY - 8), (down, 0)):
        rows = pl.ds(at, 8)
        for f in range(WAVES):
            copy(state.at[f, :, rows, :], to.at[pl.ds(f * NZ, NZ)])
        for m, ref in enumerate((lame, shear, buoyancy)):
            copy(ref.at[:, rows, :], to.at[pl.ds((WAVES + m) * NZ, NZ)])
    lane = lanes_of((8, 128))
    mine = jnp.zeros((8, 128), jnp.int32)
    for k in range(4):
        mine = jnp.where(lane == k, cells[0, k], mine)
    up[PLANES] = mine.astype(F32)
    down[PLANES] = mine.astype(F32)
    for made in copies:
        made.wait()


def edges_kernel(state, lame, shear, buoyancy, below, above, own, right, left):
    lane = lanes_of((8, 128))
    planes = [state.at[f] for f in range(WAVES)] + [lame, shear, buoyancy]
    for group in range(GROUPS):
        tails, heads = [], []
        for f, field in enumerate(planes):
            tail = jnp.zeros((8, 128), F32)
            head = jnp.zeros((8, 128), F32)
            for z in range(NZ):
                if group == 0:
                    plane = below[f * NZ + z]
                elif group == GROUPS - 1:
                    plane = above[f * NZ + z]
                else:
                    plane = field[z, 8 * group - 8 : 8 * group, :]
                tail = jnp.where(lane // 8 == 2 * z, roll(plane, 16 * z - 120), tail)
                head = jnp.where(lane // 8 == 2 * z + 1, roll(plane, 16 * z + 8), head)
            tails.append(tail)
            heads.append(head)
        for pair in range(FIELDS // 2):
            right[pair * GROUPS + group] = tails[2 * pair] + roll(tails[2 * pair + 1], 8)
            left[pair * GROUPS + group] = heads[2 * pair] + roll(heads[2 * pair + 1], -8)
    row = rows_of((8, 128))
    cells = jnp.where(row == 0, below[PLANES], jnp.where(row == 1, own[PLANES], above[PLANES]))
    right[EDGES] = cells
    left[EDGES] = cells


def column_of(row_vector):
    return jnp.transpose(jnp.broadcast_to(row_vector, (128, 128)))


def source_kernel(residual, counts, stations, table, send, held, totals, sems):
    copies = [pltpu.make_async_copy(residual.at[c], held.at[c], sems.at[c]) for c in range(3)]
    for copy in copies:
        copy.start()
    rows = held.shape[1]
    pad = jnp.zeros((1, 128 - rows), F32)
    count = column_of(jnp.concatenate([counts[...].astype(F32), pad], 1))[:rows]
    station_row = jnp.concatenate([stations[...], jnp.full((1, 128 - rows), -1, jnp.int32)], 1)
    station = column_of(station_row.astype(F32))[:rows].astype(jnp.int32)
    lane = lanes_of((rows, 128))
    total = jnp.zeros((rows, 128), F32)
    live = jnp.concatenate(
        [
            jnp.where((lane + 128 * g).astype(F32) < count, 1.0, 0.0).astype(BF16)
            for g in range(SAMPLES // 128)
        ],
        1,
    )
    for c in range(3):
        copies[c].wait()
        masked = held[c] * live
        product = jnp.dot(masked, table[...], preferred_element_type=F32)
        total = jnp.where(lane // 8 % 3 == c, product, total)
    mine = jnp.where(lane // 24 == station % 4, total, 0.0)
    mine = jnp.concatenate([mine, jnp.zeros((128 - rows, 128), F32)], 0)
    owner = rows_of((128, 128))
    names = jnp.where(owner == station_row // 4, 1.0, 0.0)
    by_owner = jnp.dot(
        names, mine, preferred_element_type=F32, precision=lax.Precision.HIGHEST
    )
    totals[0:24, :] = jnp.zeros((24, 128), F32)
    totals[152:176, :] = jnp.zeros((24, 128), F32)
    totals[24:152, :] = by_owner
    lane = lanes_of((128, 128))
    tile_y = owner % N_GY
    for d, (dx, dy) in enumerate(AROUND):
        near = totals[pl.ds(24 + dx * N_GY + dy, 128), :]
        inside = (tile_y + dy >= 0) & (tile_y + dy < N_GY) & (lane < 96)
        near = jnp.where(inside, near, 0.0)
        if d < 3:
            near = jnp.where(lane < 96, near, roll(by_owner, 96 - 32 * d))
        send[pl.ds(d, 128, stride=8), :] = near


def step_kernel(
    where_ref,
    state,
    lame,
    shear,
    buoyancy,
    own_right,
    own_left,
    from_left,
    from_right,
    from_below,
    from_above,
    forward_dilation,
    forward_shear,
    sources,
    tile_map,
    out,
    send,
    main_v,
    main_s,
    strip_v,
    strip_s,
    mats,
    mat_strips,
    fd,
    fs,
    edges,
    plane_src,
    kern,
    sems,
):
    top = PAD + HALO + CY
    wave_planes = WAVES * NZ
    copies = []

    def copy(src, dst):
        made = pltpu.make_async_copy(src, dst, sems.at[len(copies)])
        made.start()
        copies.append(made)

    for i, ref in enumerate((own_right, own_left, from_left, from_right)):
        copy(ref, edges.at[i])
    for f in range(WAVES):
        ref, p = (main_v, f * NZ) if f < 3 else (main_s, (f - 3) * NZ)
        copy(state.at[f], ref.at[pl.ds(p, NZ), pl.ds(PAD + HALO, CY), :])
    for m, ref in enumerate((lame, shear, buoyancy)):
        copy(ref, mats.at[pl.ds(m * NZ, NZ), pl.ds(HALO, CY), :])
    for ref, at in ((from_below, PAD), (from_above, top)):
        copy(ref.at[pl.ds(0, 3 * NZ)], main_v.at[:, pl.ds(at, 8), :])
        copy(ref.at[pl.ds(3 * NZ, 6 * NZ)], main_s.at[:, pl.ds(at, 8), :])
        copy(ref.at[pl.ds(wave_planes, 3 * NZ)], mats.at[:, pl.ds(at - PAD, 8), :])
    copy(forward_dilation, fd)
    copy(forward_shear, fs)

    zero = jnp.zeros((8, 128), F32)
    for ref in (main_v, main_s, strip_v, strip_s):
        for p in range(ref.shape[0]):
            ref[p, 0:8, :] = zero
            ref[p, top + 8 : top + 16, :] = zero
    for p in range(2 * NZ):
        for g in range(CY // 8):
            kern[pl.ds(p * CY + 8 * g, 8), :] = zero

    me, tile_x, tile_y = where_ref[0], where_ref[1], where_ref[2]
    lane = lanes_of((8, 128))
    row = rows_of((8, 128))

    def add_sender(i, carry):
        block = sources[pl.ds(pl.multiple_of(i * 32, 32), 32), :]
        return carry + (block[0:8] + block[8:16]) + (block[16:24] + block[24:32])

    got = lax.fori_loop(0, OWNERS // 4, add_sender, zero)
    own = zero
    for d in range(3):
        own = jnp.where(lane // 32 == d, roll(got, 32 + 32 * d)[d : d + 1], own)
    own = jnp.where((row == 0) & (lane < 96), own, 0.0)
    full = jnp.concatenate([got, own, jnp.zeros((112, 128), F32)], 0)
    turned = jnp.transpose(full)
    values = jnp.zeros((24, 128), F32)
    lane24 = lanes_of((24, 128))
    for k in range(4):
        part = turned[k * 24 : (k + 1) * 24]
        values = jnp.where(lane24 // 16 == k, roll(part, 16 * k), values)
    high, middle, low = three_parts(values)
    high, middle, low = high.astype(F32), middle.astype(F32), low.astype(F32)
    values = jnp.concatenate([jnp.where(lane24 < 64, high, roll(middle, 64)), low], 1)

    for made in copies[:4]:
        made.wait()
    row16 = rows_of((16, 128))
    cells = jnp.zeros((16, 128), F32)
    for d, (dx, dy) in enumerate(AROUND + [(0, 0)]):
        line = edges[(0, 3, 2)[dx], EDGES][dy + 1 : dy + 2]
        cells = jnp.where(row16 == d, line, cells)
    turned = jnp.transpose(jnp.concatenate([cells, jnp.zeros((112, 128), F32)], 0))
    lane1 = lanes_of((1, 128))
    across = jnp.zeros((1, 128), F32)
    for k in range(4):
        across = jnp.where(lane1 // 16 == k, roll(turned[k : k + 1], 16 * k), across)
    across = jnp.where(lane1 < 64, across, roll(across, 64)).astype(jnp.int32)
    across = jnp.concatenate([across, across], 1)
    along = jnp.concatenate([jnp.broadcast_to(cells[:, k : k + 1], (16, 256)) for k in range(4)], 0)
    along = along.astype(jnp.int32)
    at_row = rows_of((ROWS, 256)) == across // NX - tile_y * CY + HALO
    at_x = along % NX - tile_x * CX
    n = lanes_of((64, 256))
    hit = (n == at_x) & (n < 128)
    hit = hit | ((n - 128 == at_x + 8) & (n >= 128) & (n < 144))
    hit = hit | ((n - 192 == at_x - 120) & (n >= 192) & (n < 208))
    hit = jnp.where(hit, 1.0, 0.0).astype(BF16)
    hit = jnp.concatenate([hit, hit, hit, hit], 0)
    spread = jnp.concatenate(
        [jnp.where(at_row, values[i : i + 1], 0.0).astype(BF16) for i in range(24)], 0
    )
    plane_src[...] = jnp.dot(spread, hit, preferred_element_type=F32)

    low = lane // 8 % 2 == 0
    for pair in range(FIELDS // 2):
        for g in range(GROUPS):
            sr, sl, rl, rr = (edges[i, pair * GROUPS + g] for i in range(4))
            made = (
                jnp.where(low, rl, sl),
                jnp.where(low, sr, rr),
                jnp.where(low, roll(rl, -8), roll(sl, 8)),
                jnp.where(low, roll(sr, -8), roll(rr, 8)),
            )
            for i in range(4):
                at = 4 * pair + i
                if at < 6:
                    strip_v[at, PAD + 8 * g : PAD + 8 * g + 8, :] = made[i]
                elif at < 2 * WAVES:
                    strip_s[at - 6, PAD + 8 * g : PAD + 8 * g + 8, :] = made[i]
                else:
                    mat_strips[at - 2 * WAVES, 8 * g : 8 * g + 8, :] = made[i]
    for made in copies[4:]:
        made.wait()

    last = lane == 127
    first = lane == 0

    def mload(f, z, r):
        return main_v[f * NZ + z, pl.ds(r, 8), :] if f < 3 else main_s[(f - 3) * NZ + z, pl.ds(r, 8), :]

    def sload(f, side, r):
        return strip_v[2 * f + side, pl.ds(r, 8), :] if f < 3 else strip_s[2 * f - 6 + side, pl.ds(r, 8), :]

    def next_x(value, edge, z):
        return jnp.where(last, roll(edge, 127 - (16 * z + 8)), roll(value, -1))

    def prev_x(value, edge, z):
        return jnp.where(first, roll(edge, -(16 * z + 7)), roll(value, 1))

    def next_z(value):
        return jnp.where(lane < 112, roll(value, -16), 0.0)

    def prev_z(value):
        return jnp.where(lane >= 16, roll(value, 16), 0.0)

    def velocity_group(step, g):
        r = PAD + 8 * g
        edges = {(f, s): sload(f, s, r) for f in range(SXX, WAVES) for s in range(2)}
        below_xz = below_yz = zero
        zz = mload(SZZ, 0, r)
        for z in range(NZ):
            xx, xy, yy, xz, yz = (mload(f, z, r) for f in (SXX, SXY, SYY, SXZ, SYZ))
            above_zz = mload(SZZ, z + 1, r) if z < NZ - 1 else zero
            ax = (next_x(xx, edges[SXX, 1], z) - xx) + (xy - mload(SXY, z, r - 1)) + (xz - below_xz)
            ay = (xy - prev_x(xy, edges[SXY, 0], z)) + (mload(SYY, z, r + 1) - yy) + (yz - below_yz)
            az = (xz - prev_x(xz, edges[SXZ, 0], z)) + (yz - mload(SYZ, z, r - 1)) + (above_zz - zz)
            below_xz, below_yz, zz = xz, yz, above_zz
            hb = H * mats[2 * NZ + z, pl.ds(r - PAD, 8), :]
            for c, a in enumerate((ax, ay, az)):
                if z == 0:
                    at = pl.multiple_of((c * STEPS + step) * ROWS + 8 * g, 8)
                    a = a + plane_src[pl.ds(at, 8), 0:128]
                main_v[c * NZ + z, pl.ds(r, 8), :] = mload(c, z, r) + hb * a
        for side in range(2):
            xx, yy, zz, xy, xz, yz = (edges[f, side] for f in (SXX, SYY, SZZ, SXY, SXZ, SYZ))
            ax = (roll(xx, -1) - xx) + (xy - sload(SXY, side, r - 1)) + (xz - prev_z(xz))
            ay = (xy - roll(xy, 1)) + (sload(SYY, side, r + 1) - yy) + (yz - prev_z(yz))
            az = (xz - roll(xz, 1)) + (yz - sload(SYZ, side, r - 1)) + (next_z(zz) - zz)
            hb = H * mat_strips[2 * 2 + side, pl.ds(r - PAD, 8), :]
            for c, a in enumerate((ax, ay, az)):
                at = pl.multiple_of((c * STEPS + step) * ROWS + 8 * g, 8)
                src = plane_src[pl.ds(at, 8), 128:256]
                src = jnp.where(lane < 16, roll(src, 64) if side else src, 0.0)
                strip_v[2 * c + side, pl.ds(r, 8), :] = sload(c, side, r) + hb * (a + src)

    def stress_group(g, forward):
        r = PAD + 8 * g
        edges = {(f, s): sload(f, s, r) for f in range(3) for s in range(2)}
        vx, vy = mload(VX, 0, r), mload(VY, 0, r)
        below_vz = zero
        for z in range(NZ):
            vz = mload(VZ, z, r)
            above_vx = mload(VX, z + 1, r) if z < NZ - 1 else zero
            above_vy = mload(VY, z + 1, r) if z < NZ - 1 else zero
            exx = vx - prev_x(vx, edges[VX, 0], z)
            eyy = vy - mload(VY, z, r - 1)
            ezz = vz - below_vz
            dilation = exx + eyy + ezz
            exy = (mload(VX, z, r + 1) - vx) + (next_x(vy, edges[VY, 1], z) - vy)
            exz = (above_vx - vx) + (next_x(vz, edges[VZ, 1], z) - vz)
            eyz = (above_vy - vy) + (mload(VZ, z, r + 1) - vz)
            vx, vy, below_vz = above_vx, above_vy, vz
            pressure = H * mats[z, pl.ds(r - PAD, 8), :] * dilation
            hm = H * mats[NZ + z, pl.ds(r - PAD, 8), :]
            hm2 = hm + hm
            for f, change in (
                (SXX, pressure + hm2 * exx),
                (SYY, pressure + hm2 * eyy),
                (SZZ, pressure + hm2 * ezz),
                (SXY, hm * exy),
                (SXZ, hm * exz),
                (SYZ, hm * eyz),
            ):
                main_s[(f - 3) * NZ + z, pl.ds(r, 8), :] = mload(f, z, r) + change
            if forward is not None:
                for k, strain in ((0, dilation), (1, exy)):
                    at = pl.ds((k * NZ + z) * CY + 8 * (g - 1), 8)
                    kern[at, :] = kern[at, :] + forward[k][z] * (H * strain)
        for side in range(2):
            vx, vy, vz = (edges[f, side] for f in range(3))
            exx = vx - roll(vx, 1)
            eyy = vy - sload(VY, side, r - 1)
            ezz = vz - prev_z(vz)
            exy = (sload(VX, side, r + 1) - vx) + (roll(vy, -1) - vy)
            exz = (next_z(vx) - vx) + (roll(vz, -1) - vz)
            eyz = (next_z(vy) - vy) + (sload(VZ, side, r + 1) - vz)
            pressure = H * mat_strips[side, pl.ds(r - PAD, 8), :] * (exx + eyy + ezz)
            hm = H * mat_strips[2 + side, pl.ds(r - PAD, 8), :]
            hm2 = hm + hm
            for f, change in (
                (SXX, pressure + hm2 * exx),
                (SYY, pressure + hm2 * eyy),
                (SZZ, pressure + hm2 * ezz),
                (SXY, hm * exy),
                (SXZ, hm * exz),
                (SYZ, hm * eyz),
            ):
                strip_s[2 * f - 6 + side, pl.ds(r, 8), :] = sload(f, side, r) + change

    def one_step(step, carry):
        for g in range(GROUPS):
            velocity_group(step, g)
        stress_group(0, None)
        for i in range(CY // 16):
            both = [
                [ref[step, z, 16 * i : 16 * i + 16, :].astype(F32) for z in range(NZ)]
                for ref in (fd, fs)
            ]
            for half in range(2):
                part = [[v[8 * half : 8 * half + 8] for v in vs] for vs in both]
                stress_group(1 + 2 * i + half, part)
        stress_group(GROUPS - 1, None)
        return carry

    lax.fori_loop(0, STEPS, one_step, 0)

    outs = []
    for f in range(WAVES):
        ref, p = (main_v, f * NZ) if f < 3 else (main_s, (f - 3) * NZ)
        made = pltpu.make_async_copy(
            ref.at[pl.ds(p, NZ), pl.ds(PAD + HALO, CY), :], out.at[f], sems.at[f]
        )
        made.start()
        outs.append(made)

    slot = tile_map[...] // 256 * 2 + (tile_map[...] % 256 - 2 * me)
    slot = slot.astype(F32)
    line = jnp.zeros((8, 128), F32)
    for y in range(8):
        half = slot[:, 128 * (y // 4) : 128 * (y // 4) + 128]
        line = jnp.where(row == y, roll(half, -32 * (y % 4)), line)
    widen = jnp.where(lanes_of((128, 128)) // 4 == rows_of((128, 128)), 1.0, 0.0).astype(BF16)
    line = jnp.where(lane < 32, line, 0.0).astype(BF16)
    line = jnp.dot(line, widen, preferred_element_type=F32)
    place = rows_of((256, 128)).astype(F32)
    put = jnp.concatenate(
        [jnp.where(line[y : y + 1] == place, 1.0 / 16, 0.0).astype(BF16) for y in range(8)], 1
    )
    sums = []
    for y in range(8):
        parts = [kern[pl.ds(4 * y + i, 2 * NZ, stride=CY), :] for i in range(4)]
        sums.append((parts[0] + parts[1]) + (parts[2] + parts[3]))
    sums = jnp.concatenate(three_parts(jnp.concatenate(sums, 1)), 0)
    placed = lax.dot_general(put, sums, (((1,), (1,)), ((), ())), preferred_element_type=F32)
    placed = placed[:, 0:16] + placed[:, 16:32] + placed[:, 32:48]
    send[...] = jnp.concatenate([placed, jnp.zeros((256, 112), F32)], 1)
    for made in outs:
        made.wait()


def turn_kernel(got, out):
    out[...] = jnp.transpose(got[...])[0:16]


def shift(value, dx, dy):
    pairs = [
        (x * N_GY + y, (x + dx) * N_GY + y + dy)
        for x in range(N_GX)
        for y in range(N_GY)
        if 0 <= x + dx < N_GX and 0 <= y + dy < N_GY
    ]
    return lax.ppermute(value, ("gx", "gy"), pairs)


def shape(*dims):
    return jax.ShapeDtypeStruct(dims, F32)


def cost(flops, data):
    return pl.CostEstimate(flops=flops, bytes_accessed=data, transcendentals=0)


def local(
    adjoint_state,
    lame_lambda,
    shear_modulus,
    buoyancy,
    forward_dilation,
    forward_shear,
    residual,
    sample_counts,
    station_list,
    receiver_cells,
    tile_map,
):
    tile_x = lax.axis_index("gx")
    tile_y = lax.axis_index("gy")
    here = jnp.stack([tile_x * N_GY + tile_y, tile_x, tile_y]).astype(jnp.int32)
    rows_dev = residual.shape[0]

    up, down = pl.pallas_call(
        rows_kernel,
        out_shape=(shape(PLANES + 1, 8, 128), shape(PLANES + 1, 8, 128)),
        in_specs=[ANY] * 4 + [SMEM],
        out_specs=(VMEM, VMEM),
        scratch_shapes=[pltpu.SemaphoreType.DMA((24,))],
        cost_estimate=cost(0, 1 << 21),
    )(adjoint_state, lame_lambda, shear_modulus, buoyancy, receiver_cells.reshape(1, 4))
    from_below = shift(up, 0, 1)
    from_above = shift(down, 0, -1)

    send = pl.pallas_call(
        source_kernel,
        out_shape=shape(OWNERS * 8, 128),
        in_specs=[ANY, VMEM, VMEM, VMEM],
        out_specs=VMEM,
        scratch_shapes=[
            pltpu.VMEM((3, rows_dev, SAMPLES), BF16),
            pltpu.VMEM((176, 128), F32),
            pltpu.SemaphoreType.DMA((3,)),
        ],
        compiler_params=FULL,
        cost_estimate=cost(1 << 30, 1 << 22),
    )(
        jnp.transpose(residual, (1, 0, 2)),
        sample_counts.reshape(1, rows_dev),
        station_list.reshape(1, rows_dev),
        jnp.asarray(resample_table()),
    )
    sources = lax.all_to_all(send, ("gx", "gy"), 0, 0, tiled=True)

    right, left = pl.pallas_call(
        edges_kernel,
        out_shape=(shape(EDGES + 1, 8, 128), shape(EDGES + 1, 8, 128)),
        in_specs=[VMEM] * 7,
        out_specs=(VMEM, VMEM),
        cost_estimate=cost(1 << 20, 1 << 21),
    )(adjoint_state, lame_lambda, shear_modulus, buoyancy, from_below, from_above, up)
    from_left = shift(right, 1, 0)
    from_right = shift(left, -1, 0)

    wave_planes = WAVES * NZ
    reach = ROWS + 2 * PAD
    adjoint_out, send = pl.pallas_call(
        step_kernel,
        out_shape=(shape(WAVES, NZ, CY, CX), shape(256, 128)),
        in_specs=[SMEM] + [ANY] * 12 + [VMEM, VMEM],
        out_specs=(ANY, VMEM),
        scratch_shapes=[
            pltpu.VMEM((3 * NZ, reach, 128), F32),
            pltpu.VMEM((6 * NZ, reach, 128), F32),
            pltpu.VMEM((6, reach, 128), F32),
            pltpu.VMEM((12, reach, 128), F32),
            pltpu.VMEM((3 * NZ, ROWS, 128), F32),
            pltpu.VMEM((6, ROWS, 128), F32),
            pltpu.VMEM((STEPS, NZ, CY, CX), BF16),
            pltpu.VMEM((STEPS, NZ, CY, CX), BF16),
            pltpu.VMEM((4, EDGES + 1, 8, 128), F32),
            pltpu.VMEM((24 * ROWS, 256), F32),
            pltpu.VMEM((2 * NZ * CY, 128), F32),
            pltpu.SemaphoreType.DMA((32,)),
        ],
        compiler_params=FULL,
        cost_estimate=cost(1 << 27, 1 << 23),
    )(
        here,
        adjoint_state,
        lame_lambda,
        shear_modulus,
        buoyancy,
        right,
        left,
        from_left,
        from_right,
        from_below,
        from_above,
        forward_dilation,
        forward_shear,
        sources,
        tile_map.reshape(1, 256),
    )
    got = lax.all_to_all(send, ("gx", "gy"), 0, 0, tiled=True)
    kernels = pl.pallas_call(
        turn_kernel,
        out_shape=shape(16, 256),
        in_specs=[VMEM],
        out_specs=VMEM,
    )(got)
    return kernels.reshape(2, NZ, 256), adjoint_out


def solution(mesh):
    in_specs = (
        P(None, None, "gy", "gx"),
        P(None, "gy", "gx"),
        P(None, "gy", "gx"),
        P(None, "gy", "gx"),
        P(None, None, "gy", "gx"),
        P(None, None, "gy", "gx"),
        P(("gx", "gy"), None, None),
        P(("gx", "gy")),
        P(("gx", "gy")),
        P(("gx", "gy")),
        P(("gx", "gy")),
    )
    out_specs = (P(None, None, ("gx", "gy")), P(None, None, "gy", "gx"))
    return jax.shard_map(local, mesh=mesh, in_specs=in_specs, out_specs=out_specs, check_vma=False)
```

```python
import math

import jax
import jax.numpy as jnp
import numpy as np
from jax import lax
from jax.experimental import pallas as pl
from jax.experimental.pallas import tpu as pltpu
from jax.sharding import PartitionSpec as P

F32 = jnp.float32
BF16 = jnp.bfloat16

NZ, CY, CX = 8, 32, 128
STEPS = 8
SAMPLES = 4096
H = 0.25
N_GX, N_GY = 8, 16
OWNERS = N_GX * N_GY
NX = N_GX * CX
HALO = 8
ROWS = CY + 2 * HALO
PAD = 8
GROUPS = ROWS // 8
FIELDS = 12
WAVES = 9
PLANES = FIELDS * NZ
EDGES = FIELDS // 2 * GROUPS

AROUND = [(dx, dy) for dx in (-1, 0, 1) for dy in (-1, 0, 1) if (dx, dy) != (0, 0)]

VX, VY, VZ, SXX, SYY, SZZ, SXY, SXZ, SYZ = range(WAVES)

VMEM = pl.BlockSpec(memory_space=pltpu.VMEM)
SMEM = pl.BlockSpec(memory_space=pltpu.SMEM)
ANY = pl.BlockSpec(memory_space=pltpu.HBM)


PART = pltpu.CompilerParams(vmem_limit_bytes=24 << 20)


def lanes_of(shape):
    return lax.broadcasted_iota(jnp.int32, shape, len(shape) - 1)


def rows_of(shape):
    return lax.broadcasted_iota(jnp.int32, shape, len(shape) - 2)


def roll(value, shift):
    return pltpu.roll(value, shift % value.shape[-1], value.ndim - 1)


def three_parts(value):
    high = value.astype(BF16)
    rest = value - high.astype(F32)
    middle = rest.astype(BF16)
    low = (rest - middle.astype(F32)).astype(BF16)
    return high, middle, low


def resample_table():
    per_step = SAMPLES // STEPS
    position = np.arange(SAMPLES, dtype=np.float32) + np.float32(0.5)
    centers = (np.arange(STEPS, dtype=np.float32) + np.float32(0.5)) * np.float32(per_step)
    distance = np.abs(position[:, None] - centers[None, :]) / np.float32(per_step)
    weight = np.maximum(np.float32(0.0), np.float32(1.0) - distance)
    table = (weight / np.float32(math.sqrt(per_step))).astype(BF16)
    wide = np.zeros((SAMPLES, 128), BF16)
    wide[:, :96] = np.tile(table, (1, 12))
    return wide


def at_plane(velocity, stress, mats, f):
    if f < 3:
        return velocity, f * NZ
    if f < WAVES:
        return stress, (f - 3) * NZ
    return mats, (f - WAVES) * NZ


def rows_kernel(state, lame, shear, buoyancy, cells, velocity, stress, mats, up, down, sems):
    copies = []
    for f in range(FIELDS):
        to, p = at_plane(velocity, stress, mats, f)
        source = state.at[f] if f < WAVES else (lame, shear, buoyancy)[f - WAVES]
        to = to.at[pl.ds(p, NZ), pl.ds(PAD + HALO, CY), :]
        copies.append(pltpu.make_async_copy(source, to, sems.at[f]))
        copies[f].start()
    zero = jnp.zeros((8, 128), F32)
    for ref in (velocity, stress, mats):
        for p in range(ref.shape[0]):
            ref[p, 0:8, :] = zero
            ref[p, 56:64, :] = zero
    lane = lanes_of((8, 128))
    mine = jnp.zeros((8, 128), jnp.int32)
    for k in range(4):
        mine = jnp.where(lane == k, cells[0, k], mine)
    up[PLANES] = mine.astype(F32)
    down[PLANES] = mine.astype(F32)
    for f in range(FIELDS):
        copies[f].wait()
        ref, p = at_plane(velocity, stress, mats, f)
        for z in range(NZ):
            down[f * NZ + z] = ref[p + z, 16:24, :]
            up[f * NZ + z] = ref[p + z, 40:48, :]


def edges_kernel(v_in, s_in, m_in, below, above, own, velocity, stress, mats, right, left):
    del v_in, s_in, m_in
    lane = lanes_of((8, 128))
    for f in range(FIELDS):
        ref, p = at_plane(velocity, stress, mats, f)
        for z in range(NZ):
            ref[p + z, 8:16, :] = below[f * NZ + z]
            ref[p + z, 48:56, :] = above[f * NZ + z]
    for group in range(GROUPS):
        tails, heads = [], []
        for f in range(FIELDS):
            ref, p = at_plane(velocity, stress, mats, f)
            tail = jnp.zeros((8, 128), F32)
            head = jnp.zeros((8, 128), F32)
            for z in range(NZ):
                if group in (0, GROUPS - 1):
                    plane = (above if group else below)[f * NZ + z]
                else:
                    plane = ref[p + z, PAD + 8 * group : PAD + 8 * group + 8, :]
                tail = jnp.where(lane // 8 == 2 * z, roll(plane, 16 * z - 120), tail)
                head = jnp.where(lane // 8 == 2 * z + 1, roll(plane, 16 * z + 8), head)
            tails.append(tail)
            heads.append(head)
        for pair in range(FIELDS // 2):
            right[pair * GROUPS + group] = tails[2 * pair] + roll(tails[2 * pair + 1], 8)
            left[pair * GROUPS + group] = heads[2 * pair] + roll(heads[2 * pair + 1], -8)
    row = rows_of((8, 128))
    cells = jnp.where(row == 0, below[PLANES], jnp.where(row == 1, own[PLANES], above[PLANES]))
    right[EDGES] = cells
    left[EDGES] = cells


def column_of(row_vector):
    return jnp.transpose(jnp.broadcast_to(row_vector, (128, 128)))


def source_kernel(residual, counts, stations, table, send, held, totals, sems):
    copies = [pltpu.make_async_copy(residual.at[c], held.at[c], sems.at[c]) for c in range(3)]
    for copy in copies:
        copy.start()
    rows = held.shape[1]
    pad = jnp.zeros((1, 128 - rows), F32)
    count = column_of(jnp.concatenate([counts[...].astype(F32), pad], 1))[:rows]
    station_row = jnp.concatenate([stations[...], jnp.full((1, 128 - rows), -1, jnp.int32)], 1)
    station = column_of(station_row.astype(F32))[:rows].astype(jnp.int32)
    lane = lanes_of((rows, 128))
    total = jnp.zeros((rows, 128), F32)
    live = jnp.concatenate(
        [
            jnp.where((lane + 128 * g).astype(F32) < count, 1.0, 0.0).astype(BF16)
            for g in range(SAMPLES // 128)
        ],
        1,
    )
    for c in range(3):
        copies[c].wait()
        masked = held[c] * live
        product = jnp.dot(masked, table[...], preferred_element_type=F32)
        total = jnp.where(lane // 8 % 3 == c, product, total)
    mine = jnp.where(lane // 24 == station % 4, total, 0.0)
    mine = jnp.concatenate([mine, jnp.zeros((128 - rows, 128), F32)], 0)
    owner = rows_of((128, 128))
    names = jnp.where(owner == station_row // 4, 1.0, 0.0)
    by_owner = jnp.dot(
        names, mine, preferred_element_type=F32, precision=lax.Precision.HIGHEST
    )
    totals[0:24, :] = jnp.zeros((24, 128), F32)
    totals[152:176, :] = jnp.zeros((24, 128), F32)
    totals[24:152, :] = by_owner
    lane = lanes_of((128, 128))
    tile_y = owner % N_GY
    for d, (dx, dy) in enumerate(AROUND):
        near = totals[pl.ds(24 + dx * N_GY + dy, 128), :]
        inside = (tile_y + dy >= 0) & (tile_y + dy < N_GY) & (lane < 96)
        near = jnp.where(inside, near, 0.0)
        if d < 3:
            near = jnp.where(lane < 96, near, roll(by_owner, 96 - 32 * d))
        send[pl.ds(d, 128, stride=8), :] = near


def step_kernel(
    v_in,
    s_in,
    mats,
    own_right,
    own_left,
    from_left,
    from_right,
    forward_dilation,
    forward_shear,
    sources,
    tile_map,
    main_v,
    main_s,
    out,
    send,
    strip_v,
    strip_s,
    mat_strips,
    fd,
    fs,
    plane_src,
    kern,
    sems,
):
    del v_in, s_in
    forward_copies = [
        pltpu.make_async_copy(forward_dilation, fd, sems.at[0]),
        pltpu.make_async_copy(forward_shear, fs, sems.at[1]),
    ]
    for made in forward_copies:
        made.start()
    edges = (own_right, own_left, from_left, from_right)
    zero = jnp.zeros((8, 128), F32)
    for ref in (strip_v, strip_s):
        for p in range(ref.shape[0]):
            ref[p, 0:8, :] = zero
            ref[p, 56:64, :] = zero
    for p in range(2 * NZ):
        for g in range(CY // 8):
            kern[pl.ds(p * CY + 8 * g, 8), :] = zero

    tile_x, tile_y = lax.axis_index("gx"), lax.axis_index("gy")
    me = tile_x * N_GY + tile_y
    lane = lanes_of((8, 128))
    row = rows_of((8, 128))

    def add_sender(i, carry):
        block = sources[pl.ds(pl.multiple_of(i * 32, 32), 32), :]
        return carry + (block[0:8] + block[8:16]) + (block[16:24] + block[24:32])

    got = lax.fori_loop(0, OWNERS // 4, add_sender, zero)
    own = zero
    for d in range(3):
        own = jnp.where(lane // 32 == d, roll(got, 32 + 32 * d)[d : d + 1], own)
    own = jnp.where((row == 0) & (lane < 96), own, 0.0)
    full = jnp.concatenate([got, own, jnp.zeros((112, 128), F32)], 0)
    turned = jnp.transpose(full)
    values = jnp.zeros((24, 128), F32)
    lane24 = lanes_of((24, 128))
    for k in range(4):
        part = turned[k * 24 : (k + 1) * 24]
        values = jnp.where(lane24 // 16 == k, roll(part, 16 * k), values)
    high, middle, low = three_parts(values)
    high, middle, low = high.astype(F32), middle.astype(F32), low.astype(F32)
    values = jnp.concatenate([jnp.where(lane24 < 64, high, roll(middle, 64)), low], 1)

    row16 = rows_of((16, 128))
    cells = jnp.zeros((16, 128), F32)
    for d, (dx, dy) in enumerate(AROUND + [(0, 0)]):
        line = edges[(0, 3, 2)[dx]][EDGES][dy + 1 : dy + 2]
        cells = jnp.where(row16 == d, line, cells)
    turned = jnp.transpose(jnp.concatenate([cells, jnp.zeros((112, 128), F32)], 0))
    lane1 = lanes_of((1, 128))
    across = jnp.zeros((1, 128), F32)
    for k in range(4):
        across = jnp.where(lane1 // 16 == k, roll(turned[k : k + 1], 16 * k), across)
    across = jnp.where(lane1 < 64, across, roll(across, 64)).astype(jnp.int32)
    across = jnp.concatenate([across, across], 1)
    along = jnp.concatenate([jnp.broadcast_to(cells[:, k : k + 1], (16, 256)) for k in range(4)], 0)
    along = along.astype(jnp.int32)
    at_row = rows_of((ROWS, 256)) == across // NX - tile_y * CY + HALO
    at_x = along % NX - tile_x * CX
    n = lanes_of((64, 256))
    hit = (n == at_x) & (n < 128)
    hit = hit | ((n - 128 == at_x + 8) & (n >= 128) & (n < 144))
    hit = hit | ((n - 192 == at_x - 120) & (n >= 192) & (n < 208))
    hit = jnp.where(hit, 1.0, 0.0).astype(BF16)
    hit = jnp.concatenate([hit, hit, hit, hit], 0)
    spread = jnp.concatenate(
        [jnp.where(at_row, values[i : i + 1], 0.0).astype(BF16) for i in range(24)], 0
    )
    plane_src[...] = jnp.dot(spread, hit, preferred_element_type=F32)

    low = lane // 8 % 2 == 0
    for pair in range(FIELDS // 2):
        for g in range(GROUPS):
            sr, sl, rl, rr = (ref[pair * GROUPS + g] for ref in edges)
            made = (
                jnp.where(low, rl, sl),
                jnp.where(low, sr, rr),
                jnp.where(low, roll(rl, -8), roll(sl, 8)),
                jnp.where(low, roll(sr, -8), roll(rr, 8)),
            )
            for i in range(4):
                at = 4 * pair + i
                if at < 6:
                    strip_v[at, PAD + 8 * g : PAD + 8 * g + 8, :] = made[i]
                elif at < 2 * WAVES:
                    strip_s[at - 6, PAD + 8 * g : PAD + 8 * g + 8, :] = made[i]
                else:
                    mat_strips[at - 2 * WAVES, 8 * g : 8 * g + 8, :] = made[i]
    last = lane == 127
    first = lane == 0

    def mload(f, z, r):
        return main_v[f * NZ + z, pl.ds(r, 8), :] if f < 3 else main_s[(f - 3) * NZ + z, pl.ds(r, 8), :]

    def sload(f, side, r):
        return strip_v[2 * f + side, pl.ds(r, 8), :] if f < 3 else strip_s[2 * f - 6 + side, pl.ds(r, 8), :]

    def next_x(value, edge, z):
        return jnp.where(last, roll(edge, 127 - (16 * z + 8)), roll(value, -1))

    def prev_x(value, edge, z):
        return jnp.where(first, roll(edge, -(16 * z + 7)), roll(value, 1))

    def next_z(value):
        return jnp.where(lane < 112, roll(value, -16), 0.0)

    def prev_z(value):
        return jnp.where(lane >= 16, roll(value, 16), 0.0)

    def velocity_group(step, g):
        r = PAD + 8 * g
        edges = {(f, s): sload(f, s, r) for f in range(SXX, WAVES) for s in range(2)}
        below_xz = below_yz = zero
        zz = mload(SZZ, 0, r)
        for z in range(NZ):
            xx, xy, yy, xz, yz = (mload(f, z, r) for f in (SXX, SXY, SYY, SXZ, SYZ))
            above_zz = mload(SZZ, z + 1, r) if z < NZ - 1 else zero
            ax = (next_x(xx, edges[SXX, 1], z) - xx) + (xy - mload(SXY, z, r - 1)) + (xz - below_xz)
            ay = (xy - prev_x(xy, edges[SXY, 0], z)) + (mload(SYY, z, r + 1) - yy) + (yz - below_yz)
            az = (xz - prev_x(xz, edges[SXZ, 0], z)) + (yz - mload(SYZ, z, r - 1)) + (above_zz - zz)
            below_xz, below_yz, zz = xz, yz, above_zz
            hb = H * mats[2 * NZ + z, pl.ds(r, 8), :]
            for c, a in enumerate((ax, ay, az)):
                if z == 0:
                    at = pl.multiple_of((c * STEPS + step) * ROWS + 8 * g, 8)
                    a = a + plane_src[pl.ds(at, 8), 0:128]
                main_v[c * NZ + z, pl.ds(r, 8), :] = mload(c, z, r) + hb * a
        for side in range(2):
            xx, yy, zz, xy, xz, yz = (edges[f, side] for f in (SXX, SYY, SZZ, SXY, SXZ, SYZ))
            ax = (roll(xx, -1) - xx) + (xy - sload(SXY, side, r - 1)) + (xz - prev_z(xz))
            ay = (xy - roll(xy, 1)) + (sload(SYY, side, r + 1) - yy) + (yz - prev_z(yz))
            az = (xz - roll(xz, 1)) + (yz - sload(SYZ, side, r - 1)) + (next_z(zz) - zz)
            hb = H * mat_strips[2 * 2 + side, pl.ds(r - PAD, 8), :]
            for c, a in enumerate((ax, ay, az)):
                at = pl.multiple_of((c * STEPS + step) * ROWS + 8 * g, 8)
                src = plane_src[pl.ds(at, 8), 128:256]
                src = jnp.where(lane < 16, roll(src, 64) if side else src, 0.0)
                strip_v[2 * c + side, pl.ds(r, 8), :] = sload(c, side, r) + hb * (a + src)

    def stress_group(g, forward, strips):
        r = PAD + 8 * g
        edges = {(f, s): sload(f, s, r) for f in range(3) for s in range(2)}
        vx, vy = mload(VX, 0, r), mload(VY, 0, r)
        below_vz = zero
        for z in range(NZ):
            vz = mload(VZ, z, r)
            above_vx = mload(VX, z + 1, r) if z < NZ - 1 else zero
            above_vy = mload(VY, z + 1, r) if z < NZ - 1 else zero
            exx = vx - prev_x(vx, edges[VX, 0], z)
            eyy = vy - mload(VY, z, r - 1)
            ezz = vz - below_vz
            dilation = exx + eyy + ezz
            exy = (mload(VX, z, r + 1) - vx) + (next_x(vy, edges[VY, 1], z) - vy)
            exz = (above_vx - vx) + (next_x(vz, edges[VZ, 1], z) - vz)
            eyz = (above_vy - vy) + (mload(VZ, z, r + 1) - vz)
            vx, vy, below_vz = above_vx, above_vy, vz
            pressure = H * mats[z, pl.ds(r, 8), :] * dilation
            hm = H * mats[NZ + z, pl.ds(r, 8), :]
            hm2 = hm + hm
            for f, change in (
                (SXX, pressure + hm2 * exx),
                (SYY, pressure + hm2 * eyy),
                (SZZ, pressure + hm2 * ezz),
                (SXY, hm * exy),
                (SXZ, hm * exz),
                (SYZ, hm * eyz),
            ):
                main_s[(f - 3) * NZ + z, pl.ds(r, 8), :] = mload(f, z, r) + change
            if forward is not None:
                for k, strain in ((0, dilation), (1, exy)):
                    at = pl.ds((k * NZ + z) * CY + 8 * (g - 1), 8)
                    kern[at, :] = kern[at, :] + forward[k][z] * (H * strain)
        for side in range(2 if strips else 0):
            vx, vy, vz = (edges[f, side] for f in range(3))
            exx = vx - roll(vx, 1)
            eyy = vy - sload(VY, side, r - 1)
            ezz = vz - prev_z(vz)
            exy = (sload(VX, side, r + 1) - vx) + (roll(vy, -1) - vy)
            exz = (next_z(vx) - vx) + (roll(vz, -1) - vz)
            eyz = (next_z(vy) - vy) + (sload(VZ, side, r + 1) - vz)
            pressure = H * mat_strips[side, pl.ds(r - PAD, 8), :] * (exx + eyy + ezz)
            hm = H * mat_strips[2 + side, pl.ds(r - PAD, 8), :]
            hm2 = hm + hm
            for f, change in (
                (SXX, pressure + hm2 * exx),
                (SYY, pressure + hm2 * eyy),
                (SZZ, pressure + hm2 * ezz),
                (SXY, hm * exy),
                (SXZ, hm * exz),
                (SYZ, hm * eyz),
            ):
                strip_s[2 * f - 6 + side, pl.ds(r, 8), :] = sload(f, side, r) + change

    def stresses(step, halos):
        if halos:
            stress_group(0, None, True)
        for i in range(CY // 16):
            both = [
                [ref[step, z, 16 * i : 16 * i + 16, :].astype(F32) for z in range(NZ)]
                for ref in (fd, fs)
            ]
            for half in range(2):
                part = [[v[8 * half : 8 * half + 8] for v in vs] for vs in both]
                stress_group(1 + 2 * i + half, part, halos)
        if halos:
            stress_group(GROUPS - 1, None, True)

    def one_step(step, carry):
        for g in range(GROUPS):
            velocity_group(step, g)
        stresses(step, True)
        return carry

    for made in forward_copies:
        made.wait()
    lax.fori_loop(0, STEPS - 1, one_step, 0)
    for g in range(GROUPS):
        velocity_group(STEPS - 1, g)
    outs = []

    def deliver(f):
        ref, p = at_plane(main_v, main_s, None, f)
        made = pltpu.make_async_copy(
            ref.at[pl.ds(p, NZ), pl.ds(PAD + HALO, CY), :], out.at[f], sems.at[2 + f]
        )
        made.start()
        outs.append(made)

    for f in range(3):
        deliver(f)
    stresses(STEPS - 1, False)
    for f in range(3, WAVES):
        deliver(f)

    slot = tile_map[...] // 256 * 2 + (tile_map[...] % 256 - 2 * me)
    slot = slot.astype(F32)
    line = jnp.zeros((8, 128), F32)
    for y in range(8):
        half = slot[:, 128 * (y // 4) : 128 * (y // 4) + 128]
        line = jnp.where(row == y, roll(half, -32 * (y % 4)), line)
    widen = jnp.where(lanes_of((128, 128)) // 4 == rows_of((128, 128)), 1.0, 0.0).astype(BF16)
    line = jnp.where(lane < 32, line, 0.0).astype(BF16)
    line = jnp.dot(line, widen, preferred_element_type=F32)
    place = rows_of((256, 128)).astype(F32)
    put = jnp.concatenate(
        [jnp.where(line[y : y + 1] == place, 1.0 / 16, 0.0).astype(BF16) for y in range(8)], 1
    )
    sums = []
    for y in range(8):
        parts = [kern[pl.ds(4 * y + i, 2 * NZ, stride=CY), :] for i in range(4)]
        sums.append((parts[0] + parts[1]) + (parts[2] + parts[3]))
    sums = jnp.concatenate(three_parts(jnp.concatenate(sums, 1)), 0)
    placed = lax.dot_general(put, sums, (((1,), (1,)), ((), ())), preferred_element_type=F32)
    placed = placed[:, 0:16] + placed[:, 16:32] + placed[:, 32:48]
    send[...] = jnp.concatenate([placed, jnp.zeros((256, 112), F32)], 1)
    for made in outs:
        made.wait()


def turn_kernel(got, out):
    out[...] = jnp.transpose(got[...])[0:16]


def shift(value, dx, dy):
    pairs = [
        (x * N_GY + y, (x + dx) * N_GY + y + dy)
        for x in range(N_GX)
        for y in range(N_GY)
        if 0 <= x + dx < N_GX and 0 <= y + dy < N_GY
    ]
    return lax.ppermute(value, ("gx", "gy"), pairs)


def shape(*dims):
    return jax.ShapeDtypeStruct(dims, F32)


def cost(flops, data):
    return pl.CostEstimate(flops=flops, bytes_accessed=data, transcendentals=0)


def local(
    adjoint_state,
    lame_lambda,
    shear_modulus,
    buoyancy,
    forward_dilation,
    forward_shear,
    residual,
    sample_counts,
    station_list,
    receiver_cells,
    tile_map,
):
    rows_dev = residual.shape[0]
    in_hbm = lambda value: pltpu.with_memory_space_constraint(value, pltpu.HBM)
    adjoint_state, lame_lambda, shear_modulus, buoyancy, forward_dilation, forward_shear = (
        in_hbm(value)
        for value in (
            adjoint_state,
            lame_lambda,
            shear_modulus,
            buoyancy,
            forward_dilation,
            forward_shear,
        )
    )

    reach = ROWS + 2 * PAD
    held = (shape(3 * NZ, reach, 128), shape(6 * NZ, reach, 128), shape(3 * NZ, reach, 128))
    velocity, stress, mats, up, down = pl.pallas_call(
        rows_kernel,
        out_shape=held + (shape(PLANES + 1, 8, 128), shape(PLANES + 1, 8, 128)),
        in_specs=[ANY] * 4 + [SMEM],
        out_specs=(VMEM,) * 5,
        scratch_shapes=[pltpu.SemaphoreType.DMA((FIELDS,))],
        compiler_params=PART,
        cost_estimate=cost(0, 1 << 21),
    )(adjoint_state, lame_lambda, shear_modulus, buoyancy, in_hbm(receiver_cells.reshape(1, 4)))
    from_below = shift(up, 0, 1)
    from_above = shift(down, 0, -1)

    send = pl.pallas_call(
        source_kernel,
        out_shape=shape(OWNERS * 8, 128),
        in_specs=[ANY, VMEM, VMEM, VMEM],
        out_specs=VMEM,
        scratch_shapes=[
            pltpu.VMEM((3, rows_dev, SAMPLES), BF16),
            pltpu.VMEM((176, 128), F32),
            pltpu.SemaphoreType.DMA((3,)),
        ],
        compiler_params=PART,
        cost_estimate=cost(1 << 30, 1 << 22),
    )(
        in_hbm(jnp.transpose(residual, (1, 0, 2))),
        in_hbm(sample_counts.reshape(1, rows_dev)),
        in_hbm(station_list.reshape(1, rows_dev)),
        jnp.asarray(resample_table()),
    )
    send = in_hbm(send)
    sources = lax.all_to_all(send, ("gx", "gy"), 0, 0, tiled=True)

    velocity, stress, mats, right, left = pl.pallas_call(
        edges_kernel,
        out_shape=held + (shape(EDGES + 1, 8, 128), shape(EDGES + 1, 8, 128)),
        in_specs=[VMEM] * 6,
        out_specs=(VMEM,) * 5,
        input_output_aliases={0: 0, 1: 1, 2: 2},
        compiler_params=PART,
        cost_estimate=cost(1 << 20, 1 << 21),
    )(velocity, stress, mats, from_below, from_above, up)
    from_left = shift(right, 1, 0)
    from_right = shift(left, -1, 0)

    _, _, adjoint_out, send = pl.pallas_call(
        step_kernel,
        out_shape=held[:2] + (shape(WAVES, NZ, CY, CX), shape(256, 128)),
        in_specs=[VMEM] * 7 + [ANY] * 2 + [VMEM, VMEM],
        out_specs=(VMEM, VMEM, ANY, VMEM),
        input_output_aliases={0: 0, 1: 1},
        scratch_shapes=[
            pltpu.VMEM((6, reach, 128), F32),
            pltpu.VMEM((12, reach, 128), F32),
            pltpu.VMEM((6, ROWS, 128), F32),
            pltpu.VMEM((STEPS, NZ, CY, CX), BF16),
            pltpu.VMEM((STEPS, NZ, CY, CX), BF16),
            pltpu.VMEM((24 * ROWS, 256), F32),
            pltpu.VMEM((2 * NZ * CY, 128), F32),
            pltpu.SemaphoreType.DMA((2 + WAVES,)),
        ],
        compiler_params=PART,
        cost_estimate=cost(1 << 27, 1 << 23),
    )(
        velocity,
        stress,
        mats,
        right,
        left,
        from_left,
        from_right,
        forward_dilation,
        forward_shear,
        sources,
        tile_map.reshape(1, 256),
    )
    got = lax.all_to_all(send, ("gx", "gy"), 0, 0, tiled=True)
    kernels = pl.pallas_call(
        turn_kernel,
        out_shape=shape(16, 256),
        in_specs=[VMEM],
        out_specs=VMEM,
    )(got)
    return kernels.reshape(2, NZ, 256), adjoint_out


def solution(mesh):
    in_specs = (
        P(None, None, "gy", "gx"),
        P(None, "gy", "gx"),
        P(None, "gy", "gx"),
        P(None, "gy", "gx"),
        P(None, None, "gy", "gx"),
        P(None, None, "gy", "gx"),
        P(("gx", "gy"), None, None),
        P(("gx", "gy")),
        P(("gx", "gy")),
        P(("gx", "gy")),
        P(("gx", "gy")),
    )
    out_specs = (P(None, None, ("gx", "gy")), P(None, None, "gy", "gx"))
    return jax.shard_map(local, mesh=mesh, in_specs=in_specs, out_specs=out_specs, check_vma=False)
```

```python
import math

import jax
import jax.numpy as jnp
import numpy as np
from jax import lax
from jax.experimental import pallas as pl
from jax.experimental.pallas import tpu as pltpu
from jax.sharding import PartitionSpec as P

F32 = jnp.float32
BF16 = jnp.bfloat16

NZ, CY, CX = 8, 32, 128
STEPS = 8
SAMPLES = 4096
H = 0.25
N_GX, N_GY = 8, 16
OWNERS = N_GX * N_GY
NX = N_GX * CX
HALO = 8
ROWS = CY + 2 * HALO
GROUPS = ROWS // 8
FIELDS = 12
WAVES = 9
PLANES = FIELDS * NZ
EDGES = FIELDS // 2 * GROUPS

AROUND = [(dx, dy) for dx in (-1, 0, 1) for dy in (-1, 0, 1) if (dx, dy) != (0, 0)]

VX, VY, VZ, SXX, SYY, SZZ, SXY, SXZ, SYZ = range(WAVES)

VMEM = pl.BlockSpec(memory_space=pltpu.VMEM)
SMEM = pl.BlockSpec(memory_space=pltpu.SMEM)
ANY = pl.BlockSpec(memory_space=pltpu.HBM)


PART = pltpu.CompilerParams(vmem_limit_bytes=24 << 20)


def lanes_of(shape):
    return lax.broadcasted_iota(jnp.int32, shape, len(shape) - 1)


def rows_of(shape):
    return lax.broadcasted_iota(jnp.int32, shape, len(shape) - 2)


def roll(value, shift):
    return pltpu.roll(value, shift % value.shape[-1], value.ndim - 1)


def three_parts(value):
    high = value.astype(BF16)
    rest = value - high.astype(F32)
    middle = rest.astype(BF16)
    low = (rest - middle.astype(F32)).astype(BF16)
    return high, middle, low


def resample_table():
    per_step = SAMPLES // STEPS
    position = np.arange(SAMPLES, dtype=np.float32) + np.float32(0.5)
    centers = (np.arange(STEPS, dtype=np.float32) + np.float32(0.5)) * np.float32(per_step)
    distance = np.abs(position[:, None] - centers[None, :]) / np.float32(per_step)
    weight = np.maximum(np.float32(0.0), np.float32(1.0) - distance)
    table = (weight / np.float32(math.sqrt(per_step))).astype(BF16)
    wide = np.zeros((SAMPLES, 128), BF16)
    wide[:, :96] = np.tile(table, (1, 12))
    return wide


def at_plane(velocity, stress, mats, f):
    if f < 3:
        return velocity, f * NZ
    if f < WAVES:
        return stress, (f - 3) * NZ
    return mats, (f - WAVES) * NZ


def first_kernel(
    state,
    lame,
    shear,
    buoyancy,
    cells,
    residual,
    counts,
    stations,
    weights,
    velocity,
    stress,
    mats,
    up,
    down,
    by_owner,
    table,
    held,
    sems,
):
    copies = []
    for f in range(FIELDS):
        to, p = at_plane(velocity, stress, mats, f)
        source = state.at[f] if f < WAVES else (lame, shear, buoyancy)[f - WAVES]
        to = to.at[pl.ds(p, NZ), pl.ds(HALO, CY), :]
        copies.append(pltpu.make_async_copy(source, to, sems.at[f]))
        copies[f].start()
    table_copy = pltpu.make_async_copy(weights, table, sems.at[FIELDS])
    table_copy.start()
    rows_in = [
        pltpu.make_async_copy(residual.at[c], held.at[c], sems.at[FIELDS + 1 + c]) for c in range(3)
    ]
    for copy in rows_in:
        copy.start()
    lane = lanes_of((8, 128))
    mine = jnp.zeros((8, 128), jnp.int32)
    for k in range(4):
        mine = jnp.where(lane == k, cells[0, k], mine)
    up[PLANES] = mine.astype(F32)
    down[PLANES] = mine.astype(F32)
    rows = held.shape[1]
    pad = jnp.zeros((1, 128 - rows), F32)
    count = column_of(jnp.concatenate([counts[...].astype(F32), pad], 1))[:rows]
    station_row = jnp.concatenate([stations[...], jnp.full((1, 128 - rows), -1, jnp.int32)], 1)
    station = column_of(station_row.astype(F32))[:rows].astype(jnp.int32)
    for f in range(FIELDS):
        copies[f].wait()
        ref, p = at_plane(velocity, stress, mats, f)
        for z in range(NZ):
            down[f * NZ + z] = ref[p + z, 8:16, :]
            up[f * NZ + z] = ref[p + z, 32:40, :]
    table_copy.wait()
    by_owner[...] = sums_by_owner(rows_in, held, table, count, station, station_row)


def edges_kernel(v_in, s_in, m_in, below, above, own, velocity, stress, mats, right, left):
    del v_in, s_in, m_in
    lane = lanes_of((8, 128))
    for f in range(FIELDS):
        ref, p = at_plane(velocity, stress, mats, f)
        for z in range(NZ):
            if f < WAVES:
                ref[p + z, 0:8, :] = below[f * NZ + z]
                ref[p + z, 40:48, :] = above[f * NZ + z]
            else:
                ref[p + z, 0:8, :] = H * below[f * NZ + z]
                ref[p + z, 8:40, :] = H * ref[p + z, 8:40, :]
                ref[p + z, 40:48, :] = H * above[f * NZ + z]
    for group in range(GROUPS):
        tails, heads = [], []
        for f in range(FIELDS):
            ref, p = at_plane(velocity, stress, mats, f)
            tail = jnp.zeros((8, 128), F32)
            head = jnp.zeros((8, 128), F32)
            for z in range(NZ):
                plane = ref[p + z, 8 * group : 8 * group + 8, :]
                tail = jnp.where(lane // 8 == 2 * z, roll(plane, 16 * z - 120), tail)
                head = jnp.where(lane // 8 == 2 * z + 1, roll(plane, 16 * z + 8), head)
            tails.append(tail)
            heads.append(head)
        for pair in range(FIELDS // 2):
            right[pair * GROUPS + group] = tails[2 * pair] + roll(tails[2 * pair + 1], 8)
            left[pair * GROUPS + group] = heads[2 * pair] + roll(heads[2 * pair + 1], -8)
    row = rows_of((8, 128))
    cells = jnp.where(row == 0, below[PLANES], jnp.where(row == 1, own[PLANES], above[PLANES]))
    right[EDGES] = cells
    left[EDGES] = cells


def column_of(row_vector):
    return jnp.transpose(jnp.broadcast_to(row_vector, (128, 128)))


def sums_by_owner(rows_in, held, table, count, station, station_row):
    rows = held.shape[1]
    lane = lanes_of((rows, 128))
    total = jnp.zeros((rows, 128), F32)
    live = jnp.concatenate(
        [
            jnp.where((lane + 128 * g).astype(F32) < count, 1.0, 0.0).astype(BF16)
            for g in range(SAMPLES // 128)
        ],
        1,
    )
    for c in range(3):
        rows_in[c].wait()
        product = jnp.dot(held[c] * live, table[...], preferred_element_type=F32)
        total = jnp.where(lane // 8 % 3 == c, product, total)
    mine = jnp.where(lane // 24 == station % 4, total, 0.0)
    mine = jnp.concatenate([mine, jnp.zeros((128 - rows, 128), F32)], 0)
    names = jnp.where(rows_of((128, 128)) == station_row // 4, 1.0, 0.0)
    return jnp.dot(names, mine, preferred_element_type=F32, precision=lax.Precision.HIGHEST)


def send_kernel(by_owner, send, made_send, totals, sems):
    totals[0:24, :] = jnp.zeros((24, 128), F32)
    totals[152:176, :] = jnp.zeros((24, 128), F32)
    totals[24:152, :] = by_owner[...]
    lane = lanes_of((32, 128))
    tile_y = rows_of((32, 128)) % N_GY
    copies = []
    for i in range(OWNERS // 32):
        for d, (dx, dy) in enumerate(AROUND):
            near = totals[pl.ds(24 + 32 * i + dx * N_GY + dy, 32), :]
            inside = (tile_y + dy >= 0) & (tile_y + dy < N_GY) & (lane < 96)
            near = jnp.where(inside, near, 0.0)
            if d < 3:
                near = jnp.where(lane < 96, near, roll(by_owner[32 * i : 32 * i + 32], 96 - 32 * d))
            made_send[pl.ds(256 * i + d, 32, stride=8), :] = near
        part = pl.ds(256 * i, 256)
        copies.append(pltpu.make_async_copy(made_send.at[part], send.at[part], sems.at[i]))
        copies[i].start()
    for copy in copies:
        copy.wait()


def stencil_tools(main_v, main_s, strip_v, strip_s):
    lane = lanes_of((8, 128))
    last = lane == 127
    first = lane == 0

    def load(ref, p, r):
        if r < 0:
            return pltpu.roll(ref[p, 0:8, :], 1, 0)
        if r > ROWS - 8:
            return pltpu.roll(ref[p, ROWS - 8 : ROWS, :], 7, 0)
        return ref[p, r : r + 8, :]

    def mload(f, z, r):
        return load(main_v, f * NZ + z, r) if f < 3 else load(main_s, (f - 3) * NZ + z, r)

    def sload(f, side, r):
        return load(strip_v, 2 * f + side, r) if f < 3 else load(strip_s, 2 * f - 6 + side, r)

    def next_x(value, edge, z):
        return jnp.where(last, roll(edge, 127 - (16 * z + 8)), roll(value, -1))

    def prev_x(value, edge, z):
        return jnp.where(first, roll(edge, -(16 * z + 7)), roll(value, 1))

    def next_z(value):
        return jnp.where(lane < 112, roll(value, -16), 0.0)

    def prev_z(value):
        return jnp.where(lane >= 16, roll(value, 16), 0.0)

    return mload, sload, next_x, prev_x, next_z, prev_z


def stress_planes(tools, mats, main_s, kern, g, forward, update):
    mload, sload, next_x, prev_x = tools[:4]
    zero = jnp.zeros((8, 128), F32)
    r = 8 * g
    left_vx = sload(VX, 0, r)
    right_vy, right_vz = sload(VY, 1, r), sload(VZ, 1, r)
    vx, vy = mload(VX, 0, r), mload(VY, 0, r)
    below_vz = zero
    for z in range(NZ):
        vz = mload(VZ, z, r)
        above_vx = mload(VX, z + 1, r) if z < NZ - 1 else zero
        above_vy = mload(VY, z + 1, r) if z < NZ - 1 else zero
        exx = vx - prev_x(vx, left_vx, z)
        eyy = vy - mload(VY, z, r - 1)
        ezz = vz - below_vz
        dilation = exx + eyy + ezz
        exy = (mload(VX, z, r + 1) - vx) + (next_x(vy, right_vy, z) - vy)
        if forward is not None:
            for k, strain in ((0, dilation), (1, exy)):
                at = pl.ds((k * NZ + z) * CY + 8 * (g - 1), 8)
                kern[at, :] = kern[at, :] + forward[k][z] * (H * strain)
        if update:
            exz = (above_vx - vx) + (next_x(vz, right_vz, z) - vz)
            eyz = (above_vy - vy) + (mload(VZ, z, r + 1) - vz)
            pressure = mats[z, pl.ds(r, 8), :] * dilation
            hm = mats[NZ + z, pl.ds(r, 8), :]
            hm2 = hm + hm
            for f, change in (
                (SXX, pressure + hm2 * exx),
                (SYY, pressure + hm2 * eyy),
                (SZZ, pressure + hm2 * ezz),
                (SXY, hm * exy),
                (SXZ, hm * exz),
                (SYZ, hm * eyz),
            ):
                main_s[(f - 3) * NZ + z, pl.ds(r, 8), :] = mload(f, z, r) + change
        vx, vy, below_vz = above_vx, above_vy, vz


def step_kernel(
    v_in,
    s_in,
    mats,
    own_right,
    own_left,
    from_left,
    from_right,
    forward_dilation,
    forward_shear,
    sources,
    tile_map,
    main_v,
    main_s,
    send,
    strip_out,
    strip_v,
    strip_s,
    mat_strips,
    fd,
    fs,
    plane_src,
    kern,
    got_sources,
    made_send,
    sems,
):
    del v_in, s_in
    source_copy = pltpu.make_async_copy(sources, got_sources, sems.at[2 * STEPS])
    source_copy.start()

    def forward_copies(t):
        return (
            pltpu.make_async_copy(forward_dilation.at[t], fd.at[t], sems.at[t]),
            pltpu.make_async_copy(forward_shear.at[t], fs.at[t], sems.at[STEPS + t]),
        )

    for t in range(STEPS):
        for made in forward_copies(t):
            made.start()
    edges = (own_right, own_left, from_left, from_right)
    zero = jnp.zeros((8, 128), F32)
    for p in range(2 * NZ):
        for g in range(CY // 8):
            kern[pl.ds(p * CY + 8 * g, 8), :] = zero

    tile_x, tile_y = lax.axis_index("gx"), lax.axis_index("gy")
    me = tile_x * N_GY + tile_y
    lane = lanes_of((8, 128))
    row = rows_of((8, 128))

    low = lane // 8 % 2 == 0
    for pair in range(FIELDS // 2):
        for g in range(GROUPS):
            sr, sl, rl, rr = (ref[pair * GROUPS + g] for ref in edges)
            made = (
                jnp.where(low, rl, sl),
                jnp.where(low, sr, rr),
                jnp.where(low, roll(rl, -8), roll(sl, 8)),
                jnp.where(low, roll(sr, -8), roll(rr, 8)),
            )
            for i in range(4):
                at = 4 * pair + i
                if at < 6:
                    strip_v[at, 8 * g : 8 * g + 8, :] = made[i]
                elif at < 2 * WAVES:
                    strip_s[at - 6, 8 * g : 8 * g + 8, :] = made[i]
                else:
                    mat_strips[at - 2 * WAVES, 8 * g : 8 * g + 8, :] = made[i]
    def add_sender(i, carry):
        block = got_sources[pl.ds(pl.multiple_of(i * 32, 32), 32), :]
        return carry + (block[0:8] + block[8:16]) + (block[16:24] + block[24:32])

    source_copy.wait()
    got = lax.fori_loop(0, OWNERS // 4, add_sender, zero)
    own = zero
    for d in range(3):
        own = jnp.where(lane // 32 == d, roll(got, 32 + 32 * d)[d : d + 1], own)
    own = jnp.where((row == 0) & (lane < 96), own, 0.0)
    full = jnp.concatenate([got, own, jnp.zeros((112, 128), F32)], 0)
    turned = jnp.transpose(full)
    values = jnp.zeros((24, 128), F32)
    lane24 = lanes_of((24, 128))
    for k in range(4):
        part = turned[k * 24 : (k + 1) * 24]
        values = jnp.where(lane24 // 16 == k, roll(part, 16 * k), values)
    high, middle, low = three_parts(values)
    high, middle, low = high.astype(F32), middle.astype(F32), low.astype(F32)
    values = jnp.concatenate([jnp.where(lane24 < 64, high, roll(middle, 64)), low], 1)

    row16 = rows_of((16, 128))
    cells = jnp.zeros((16, 128), F32)
    for d, (dx, dy) in enumerate(AROUND + [(0, 0)]):
        line = edges[(0, 3, 2)[dx]][EDGES][dy + 1 : dy + 2]
        cells = jnp.where(row16 == d, line, cells)
    turned = jnp.transpose(jnp.concatenate([cells, jnp.zeros((112, 128), F32)], 0))
    lane1 = lanes_of((1, 128))
    across = jnp.zeros((1, 128), F32)
    for k in range(4):
        across = jnp.where(lane1 // 16 == k, roll(turned[k : k + 1], 16 * k), across)
    across = jnp.where(lane1 < 64, across, roll(across, 64)).astype(jnp.int32)
    across = jnp.concatenate([across, across], 1)
    along = jnp.concatenate([jnp.broadcast_to(cells[:, k : k + 1], (16, 256)) for k in range(4)], 0)
    along = along.astype(jnp.int32)
    at_row = rows_of((ROWS, 256)) == across // NX - tile_y * CY + HALO
    at_x = along % NX - tile_x * CX
    n = lanes_of((64, 256))
    hit = (n == at_x) & (n < 128)
    hit = hit | ((n - 128 == at_x + 8) & (n >= 128) & (n < 144))
    hit = hit | ((n - 192 == at_x - 120) & (n >= 192) & (n < 208))
    hit = jnp.where(hit, 1.0, 0.0).astype(BF16)
    hit = jnp.concatenate([hit, hit, hit, hit], 0)
    spread = jnp.concatenate(
        [jnp.where(at_row, values[i : i + 1], 0.0).astype(BF16) for i in range(24)], 0
    )
    plane_src[...] = jnp.dot(spread, hit, preferred_element_type=F32)

    tools = stencil_tools(main_v, main_s, strip_v, strip_s)
    mload, sload, next_x, prev_x, next_z, prev_z = tools

    def velocity_group(step, g):
        r = 8 * g
        edges = {(f, s): sload(f, s, r) for f in range(SXX, WAVES) for s in range(2)}
        below_xz = below_yz = zero
        zz = mload(SZZ, 0, r)
        for z in range(NZ):
            xx, xy, yy, xz, yz = (mload(f, z, r) for f in (SXX, SXY, SYY, SXZ, SYZ))
            above_zz = mload(SZZ, z + 1, r) if z < NZ - 1 else zero
            ax = (next_x(xx, edges[SXX, 1], z) - xx) + (xy - mload(SXY, z, r - 1)) + (xz - below_xz)
            ay = (xy - prev_x(xy, edges[SXY, 0], z)) + (mload(SYY, z, r + 1) - yy) + (yz - below_yz)
            az = (xz - prev_x(xz, edges[SXZ, 0], z)) + (yz - mload(SYZ, z, r - 1)) + (above_zz - zz)
            below_xz, below_yz, zz = xz, yz, above_zz
            hb = mats[2 * NZ + z, pl.ds(r, 8), :]
            for c, a in enumerate((ax, ay, az)):
                if z == 0:
                    at = pl.multiple_of((c * STEPS + step) * ROWS + 8 * g, 8)
                    a = a + plane_src[pl.ds(at, 8), 0:128]
                main_v[c * NZ + z, pl.ds(r, 8), :] = mload(c, z, r) + hb * a
        for side in range(2):
            xx, yy, zz, xy, xz, yz = (edges[f, side] for f in (SXX, SYY, SZZ, SXY, SXZ, SYZ))
            ax = (roll(xx, -1) - xx) + (xy - sload(SXY, side, r - 1)) + (xz - prev_z(xz))
            ay = (xy - roll(xy, 1)) + (sload(SYY, side, r + 1) - yy) + (yz - prev_z(yz))
            az = (xz - roll(xz, 1)) + (yz - sload(SYZ, side, r - 1)) + (next_z(zz) - zz)
            hb = mat_strips[2 * 2 + side, pl.ds(r, 8), :]
            for c, a in enumerate((ax, ay, az)):
                at = pl.multiple_of((c * STEPS + step) * ROWS + 8 * g, 8)
                src = plane_src[pl.ds(at, 8), 128:256]
                src = jnp.where(lane < 16, roll(src, 64) if side else src, 0.0)
                strip_v[2 * c + side, pl.ds(r, 8), :] = sload(c, side, r) + hb * (a + src)

    def stress_strips(g):
        r = 8 * g
        for side in range(2):
            vx, vy, vz = (sload(f, side, r) for f in range(3))
            exx = vx - roll(vx, 1)
            eyy = vy - sload(VY, side, r - 1)
            ezz = vz - prev_z(vz)
            exy = (sload(VX, side, r + 1) - vx) + (roll(vy, -1) - vy)
            exz = (next_z(vx) - vx) + (roll(vz, -1) - vz)
            eyz = (next_z(vy) - vy) + (sload(VZ, side, r + 1) - vz)
            pressure = mat_strips[side, pl.ds(r, 8), :] * (exx + eyy + ezz)
            hm = mat_strips[2 + side, pl.ds(r, 8), :]
            hm2 = hm + hm
            for f, change in (
                (SXX, pressure + hm2 * exx),
                (SYY, pressure + hm2 * eyy),
                (SZZ, pressure + hm2 * ezz),
                (SXY, hm * exy),
                (SXZ, hm * exz),
                (SYZ, hm * eyz),
            ):
                strip_s[2 * f - 6 + side, pl.ds(r, 8), :] = sload(f, side, r) + change

    def stresses(step, update):
        for made in forward_copies(step):
            made.wait()
        if update:
            stress_planes(tools, mats, main_s, kern, 0, None, True)
        for i in range(CY // 16):
            both = [
                [ref[step, z, 16 * i : 16 * i + 16, :].astype(F32) for z in range(NZ)]
                for ref in (fd, fs)
            ]
            for half in range(2):
                part = [[v[8 * half : 8 * half + 8] for v in vs] for vs in both]
                stress_planes(tools, mats, main_s, kern, 1 + 2 * i + half, part, update)
        if update:
            stress_planes(tools, mats, main_s, kern, GROUPS - 1, None, True)
            for g in range(GROUPS):
                stress_strips(g)

    def one_step(step, carry):
        for g in range(GROUPS):
            velocity_group(step, g)
        stresses(step, True)
        return carry

    lax.fori_loop(0, STEPS - 1, one_step, 0)
    for g in range(GROUPS):
        velocity_group(STEPS - 1, g)
    strip_copy = pltpu.make_async_copy(strip_v, strip_out, sems.at[2 * STEPS])
    strip_copy.start()
    stresses(STEPS - 1, False)

    slot = tile_map[...] // 256 * 2 + (tile_map[...] % 256 - 2 * me)
    slot = slot.astype(F32)
    line = jnp.zeros((8, 128), F32)
    for y in range(8):
        half = slot[:, 128 * (y // 4) : 128 * (y // 4) + 128]
        line = jnp.where(row == y, roll(half, -32 * (y % 4)), line)
    widen = jnp.where(lanes_of((128, 128)) // 4 == rows_of((128, 128)), 1.0, 0.0).astype(BF16)
    line = jnp.where(lane < 32, line, 0.0).astype(BF16)
    line = jnp.dot(line, widen, preferred_element_type=F32)
    place = rows_of((256, 128)).astype(F32)
    put = jnp.concatenate(
        [jnp.where(line[y : y + 1] == place, 1.0 / 16, 0.0).astype(BF16) for y in range(8)], 1
    )
    sums = []
    for y in range(8):
        parts = [kern[pl.ds(4 * y + i, 2 * NZ, stride=CY), :] for i in range(4)]
        sums.append((parts[0] + parts[1]) + (parts[2] + parts[3]))
    sums = jnp.concatenate(three_parts(jnp.concatenate(sums, 1)), 0)
    placed = lax.dot_general(put, sums, (((1,), (1,)), ((), ())), preferred_element_type=F32)
    placed = placed[:, 0:16] + placed[:, 16:32] + placed[:, 32:48]
    made_send[...] = jnp.concatenate([placed, jnp.zeros((256, 112), F32)], 1)
    send_copy = pltpu.make_async_copy(made_send, send, sems.at[0])
    send_copy.start()
    send_copy.wait()
    strip_copy.wait()


def finish_kernel(velocity, s_in, mats, strip_in, stress, out, strip_v, sems):
    del s_in
    pltpu.sync_copy(strip_in, strip_v)
    tools = stencil_tools(velocity, stress, strip_v, None)
    copies = []

    def deliver(f, rows, start):
        ref, p = at_plane(velocity, stress, None, f)
        made = pltpu.make_async_copy(
            ref.at[pl.ds(p, NZ), pl.ds(HALO + start, rows), :],
            out.at[f, :, pl.ds(start, rows), :],
            sems.at[len(copies)],
        )
        made.start()
        copies.append(made)

    for f in range(3):
        deliver(f, CY, 0)
    for g in range(CY // 8):
        stress_planes(tools, mats, stress, None, g + 1, None, True)
        for f in range(3, WAVES):
            deliver(f, 8, 8 * g)
    for made in copies:
        made.wait()


def turn_kernel(got, out):
    out[...] = jnp.transpose(got[...])[0:16]


def shift(value, dx, dy):
    pairs = [
        (x * N_GY + y, (x + dx) * N_GY + y + dy)
        for x in range(N_GX)
        for y in range(N_GY)
        if 0 <= x + dx < N_GX and 0 <= y + dy < N_GY
    ]
    return lax.ppermute(value, ("gx", "gy"), pairs)


def shape(*dims):
    return jax.ShapeDtypeStruct(dims, F32)


def cost(flops, data):
    return pl.CostEstimate(flops=flops, bytes_accessed=data, transcendentals=0)


def local(
    adjoint_state,
    lame_lambda,
    shear_modulus,
    buoyancy,
    forward_dilation,
    forward_shear,
    residual,
    sample_counts,
    station_list,
    receiver_cells,
    tile_map,
):
    rows_dev = residual.shape[0]
    in_hbm = lambda value: pltpu.with_memory_space_constraint(value, pltpu.HBM)
    adjoint_state, lame_lambda, shear_modulus, buoyancy, forward_dilation, forward_shear = (
        in_hbm(value)
        for value in (
            adjoint_state,
            lame_lambda,
            shear_modulus,
            buoyancy,
            forward_dilation,
            forward_shear,
        )
    )

    held = (shape(3 * NZ, ROWS, 128), shape(6 * NZ, ROWS, 128), shape(3 * NZ, ROWS, 128))
    velocity, stress, mats, up, down, by_owner = pl.pallas_call(
        first_kernel,
        out_shape=held + (shape(PLANES + 1, 8, 128), shape(PLANES + 1, 8, 128), shape(128, 128)),
        in_specs=[ANY] * 4 + [SMEM, ANY, VMEM, VMEM, ANY],
        out_specs=(VMEM,) * 6,
        scratch_shapes=[
            pltpu.VMEM((SAMPLES, 128), BF16),
            pltpu.VMEM((3, rows_dev, SAMPLES), BF16),
            pltpu.SemaphoreType.DMA((FIELDS + 4,)),
        ],
        compiler_params=PART,
        cost_estimate=cost(1 << 30, 1 << 22),
    )(
        adjoint_state,
        lame_lambda,
        shear_modulus,
        buoyancy,
        in_hbm(receiver_cells.reshape(1, 4)),
        in_hbm(jnp.transpose(residual, (1, 0, 2))),
        in_hbm(sample_counts.reshape(1, rows_dev)),
        in_hbm(station_list.reshape(1, rows_dev)),
        in_hbm(jnp.asarray(resample_table())),
    )
    from_below = shift(up, 0, 1)
    from_above = shift(down, 0, -1)

    send = pl.pallas_call(
        send_kernel,
        out_shape=pltpu.HBM((OWNERS * 8, 128), F32),
        in_specs=[VMEM],
        out_specs=ANY,
        scratch_shapes=[
            pltpu.VMEM((OWNERS * 8, 128), F32),
            pltpu.VMEM((176, 128), F32),
            pltpu.SemaphoreType.DMA((4,)),
        ],
        compiler_params=PART,
        cost_estimate=cost(1 << 20, 1 << 20),
    )(by_owner)
    sources = lax.all_to_all(send, ("gx", "gy"), 0, 0, tiled=True)

    velocity, stress, mats, right, left = pl.pallas_call(
        edges_kernel,
        out_shape=held + (shape(EDGES + 1, 8, 128), shape(EDGES + 1, 8, 128)),
        in_specs=[VMEM] * 6,
        out_specs=(VMEM,) * 5,
        input_output_aliases={0: 0, 1: 1, 2: 2},
        compiler_params=PART,
        cost_estimate=cost(1 << 20, 1 << 21),
    )(velocity, stress, mats, from_below, from_above, up)
    from_left = shift(right, 1, 0)
    from_right = shift(left, -1, 0)

    velocity, stress, send, strip_v = pl.pallas_call(
        step_kernel,
        out_shape=held[:2] + (pltpu.HBM((256, 128), F32), pltpu.HBM((6, ROWS, 128), F32)),
        in_specs=[VMEM] * 7 + [ANY] * 3 + [VMEM],
        out_specs=(VMEM, VMEM, ANY, ANY),
        input_output_aliases={0: 0, 1: 1},
        scratch_shapes=[
            pltpu.VMEM((6, ROWS, 128), F32),
            pltpu.VMEM((12, ROWS, 128), F32),
            pltpu.VMEM((6, ROWS, 128), F32),
            pltpu.VMEM((STEPS, NZ, CY, CX), BF16),
            pltpu.VMEM((STEPS, NZ, CY, CX), BF16),
            pltpu.VMEM((24 * ROWS, 256), F32),
            pltpu.VMEM((2 * NZ * CY, 128), F32),
            pltpu.VMEM((OWNERS * 8, 128), F32),
            pltpu.VMEM((256, 128), F32),
            pltpu.SemaphoreType.DMA((2 * STEPS + 1,)),
        ],
        compiler_params=PART,
        cost_estimate=cost(1 << 27, 1 << 23),
    )(
        velocity,
        stress,
        mats,
        right,
        left,
        from_left,
        from_right,
        forward_dilation,
        forward_shear,
        sources,
        in_hbm(tile_map.reshape(1, 256)),
    )
    got = lax.all_to_all(send, ("gx", "gy"), 0, 0, tiled=True)
    _, adjoint_out = pl.pallas_call(
        finish_kernel,
        out_shape=(held[1], shape(WAVES, NZ, CY, CX)),
        in_specs=[VMEM] * 3 + [ANY],
        out_specs=(VMEM, ANY),
        input_output_aliases={1: 0},
        scratch_shapes=[pltpu.VMEM((6, ROWS, 128), F32), pltpu.SemaphoreType.DMA((27,))],
        compiler_params=PART,
        cost_estimate=cost(1 << 24, 1 << 22),
    )(velocity, stress, mats, strip_v)
    kernels = pl.pallas_call(
        turn_kernel,
        out_shape=shape(16, 256),
        in_specs=[VMEM],
        out_specs=VMEM,
        compiler_params=PART,
    )(got)
    return kernels.reshape(2, NZ, 256), adjoint_out


def solution(mesh):
    in_specs = (
        P(None, None, "gy", "gx"),
        P(None, "gy", "gx"),
        P(None, "gy", "gx"),
        P(None, "gy", "gx"),
        P(None, None, "gy", "gx"),
        P(None, None, "gy", "gx"),
        P(("gx", "gy"), None, None),
        P(("gx", "gy")),
        P(("gx", "gy")),
        P(("gx", "gy")),
        P(("gx", "gy")),
    )
    out_specs = (P(None, None, ("gx", "gy")), P(None, None, "gy", "gx"))
    return jax.shard_map(local, mesh=mesh, in_specs=in_specs, out_specs=out_specs, check_vma=False)
```

```python
import math

import jax
import jax.numpy as jnp
import numpy as np
from jax import lax
from jax.experimental import pallas as pl
from jax.experimental.pallas import tpu as pltpu
from jax.sharding import PartitionSpec as P

F32 = jnp.float32
BF16 = jnp.bfloat16

NZ, CY, CX = 8, 32, 128
STEPS = 8
SAMPLES = 4096
H = 0.25
N_GX, N_GY = 8, 16
OWNERS = N_GX * N_GY
NX = N_GX * CX
HALO = 8
ROWS = CY + 2 * HALO
GROUPS = ROWS // 8
FIELDS = 12
WAVES = 9
PLANES = FIELDS * NZ
EDGES = FIELDS // 2 * GROUPS

AROUND = [(dx, dy) for dx in (-1, 0, 1) for dy in (-1, 0, 1) if (dx, dy) != (0, 0)]

VX, VY, VZ, SXX, SYY, SZZ, SXY, SXZ, SYZ = range(WAVES)

VMEM = pl.BlockSpec(memory_space=pltpu.VMEM)
SMEM = pl.BlockSpec(memory_space=pltpu.SMEM)
ANY = pl.BlockSpec(memory_space=pltpu.HBM)


PART = pltpu.CompilerParams(vmem_limit_bytes=24 << 20)


def lanes_of(shape):
    return lax.broadcasted_iota(jnp.int32, shape, len(shape) - 1)


def rows_of(shape):
    return lax.broadcasted_iota(jnp.int32, shape, len(shape) - 2)


def roll(value, shift):
    return pltpu.roll(value, shift % value.shape[-1], value.ndim - 1)


def three_parts(value):
    high = value.astype(BF16)
    rest = value - high.astype(F32)
    middle = rest.astype(BF16)
    low = (rest - middle.astype(F32)).astype(BF16)
    return high, middle, low


def resample_table():
    per_step = SAMPLES // STEPS
    position = np.arange(SAMPLES, dtype=np.float32) + np.float32(0.5)
    centers = (np.arange(STEPS, dtype=np.float32) + np.float32(0.5)) * np.float32(per_step)
    distance = np.abs(position[:, None] - centers[None, :]) / np.float32(per_step)
    weight = np.maximum(np.float32(0.0), np.float32(1.0) - distance)
    table = (weight / np.float32(math.sqrt(per_step))).astype(BF16)
    wide = np.zeros((per_step, 128), BF16)
    wide[:, :96] = np.tile(table[per_step : 2 * per_step], (1, 12))
    return wide


def at_plane(velocity, stress, mats, f):
    if f < 3:
        return velocity, f * NZ
    if f < WAVES:
        return stress, (f - 3) * NZ
    return mats, (f - WAVES) * NZ


def first_kernel(
    state,
    lame,
    shear,
    buoyancy,
    cells,
    residual,
    counts,
    stations,
    weights,
    velocity,
    stress,
    mats,
    up,
    down,
    by_owner,
    base,
    table,
    held,
    sems,
):
    weights_in = pltpu.make_async_copy(weights, base, sems.at[FIELDS])
    weights_in.start()
    copies = []
    for f in range(FIELDS):
        to, p = at_plane(velocity, stress, mats, f)
        source = state.at[f] if f < WAVES else (lame, shear, buoyancy)[f - WAVES]
        to = to.at[pl.ds(p, NZ), pl.ds(HALO, CY), :]
        copies.append(pltpu.make_async_copy(source, to, sems.at[f]))
        copies[f].start()
    rows_in = [
        pltpu.make_async_copy(residual.at[c], held.at[c], sems.at[FIELDS + 1 + c]) for c in range(3)
    ]
    for copy in rows_in:
        copy.start()
    lane = lanes_of((8, 128))
    mine = jnp.zeros((8, 128), jnp.int32)
    for k in range(4):
        mine = jnp.where(lane == k, cells[0, k], mine)
    up[PLANES] = mine.astype(F32)
    down[PLANES] = mine.astype(F32)
    rows = held.shape[1]
    pad = jnp.zeros((1, 128 - rows), F32)
    count = column_of(jnp.concatenate([counts[...].astype(F32), pad], 1))[:rows]
    station_row = jnp.concatenate([stations[...], jnp.full((1, 128 - rows), -1, jnp.int32)], 1)
    station = column_of(station_row.astype(F32))[:rows].astype(jnp.int32)
    weights_in.wait()
    per_step = SAMPLES // STEPS
    middle = base[...].astype(F32)
    slot = lanes_of((per_step, 128)) % STEPS
    for j in range(STEPS):
        moved = roll(middle, j - 1)
        if j in (0, STEPS - 1):
            moved = jnp.where(slot == STEPS - 1 - j, 0.0, moved)
        table[per_step * j : per_step * (j + 1), :] = moved.astype(BF16)
    for f in range(FIELDS):
        copies[f].wait()
        ref, p = at_plane(velocity, stress, mats, f)
        for z in range(NZ):
            down[f * NZ + z] = ref[p + z, 8:16, :]
            up[f * NZ + z] = ref[p + z, 32:40, :]
    by_owner[...] = sums_by_owner(rows_in, held, table, count, station, station_row)


def edges_kernel(v_in, s_in, m_in, below, above, own, velocity, stress, mats, right, left):
    del v_in, s_in, m_in
    lane = lanes_of((8, 128))
    for f in range(FIELDS):
        ref, p = at_plane(velocity, stress, mats, f)
        for z in range(NZ):
            if f < WAVES:
                ref[p + z, 0:8, :] = below[f * NZ + z]
                ref[p + z, 40:48, :] = above[f * NZ + z]
            else:
                ref[p + z, 0:8, :] = H * below[f * NZ + z]
                ref[p + z, 8:40, :] = H * ref[p + z, 8:40, :]
                ref[p + z, 40:48, :] = H * above[f * NZ + z]
    for group in range(GROUPS):
        tails, heads = [], []
        for f in range(FIELDS):
            ref, p = at_plane(velocity, stress, mats, f)
            tail = jnp.zeros((8, 128), F32)
            head = jnp.zeros((8, 128), F32)
            for z in range(NZ):
                plane = ref[p + z, 8 * group : 8 * group + 8, :]
                tail = jnp.where(lane // 8 == 2 * z, roll(plane, 16 * z - 120), tail)
                head = jnp.where(lane // 8 == 2 * z + 1, roll(plane, 16 * z + 8), head)
            tails.append(tail)
            heads.append(head)
        for pair in range(FIELDS // 2):
            right[pair * GROUPS + group] = tails[2 * pair] + roll(tails[2 * pair + 1], 8)
            left[pair * GROUPS + group] = heads[2 * pair] + roll(heads[2 * pair + 1], -8)
    row = rows_of((8, 128))
    cells = jnp.where(row == 0, below[PLANES], jnp.where(row == 1, own[PLANES], above[PLANES]))
    right[EDGES] = cells
    left[EDGES] = cells


def column_of(row_vector):
    return jnp.transpose(jnp.broadcast_to(row_vector, (128, 128)))


def sums_by_owner(rows_in, held, table, count, station, station_row):
    rows = held.shape[1]
    lane = lanes_of((rows, 128))
    total = jnp.zeros((rows, 128), F32)
    live = jnp.concatenate(
        [
            jnp.where((lane + 128 * g).astype(F32) < count, 1.0, 0.0).astype(BF16)
            for g in range(SAMPLES // 128)
        ],
        1,
    )
    for c in range(3):
        rows_in[c].wait()
        product = jnp.dot(held[c] * live, table[...], preferred_element_type=F32)
        total = jnp.where(lane // 8 % 3 == c, product, total)
    mine = jnp.where(lane // 24 == station % 4, total, 0.0)
    mine = jnp.concatenate([mine, jnp.zeros((128 - rows, 128), F32)], 0)
    names = jnp.where(rows_of((128, 128)) == station_row // 4, 1.0, 0.0)
    return jnp.dot(names, mine, preferred_element_type=F32, precision=lax.Precision.HIGHEST)


def send_kernel(by_owner, send, made_send, totals, sems):
    totals[0:24, :] = jnp.zeros((24, 128), F32)
    totals[152:176, :] = jnp.zeros((24, 128), F32)
    totals[24:152, :] = by_owner[...]
    lane = lanes_of((32, 128))
    tile_y = rows_of((32, 128)) % N_GY
    copies = []
    for i in range(OWNERS // 32):
        for d, (dx, dy) in enumerate(AROUND):
            near = totals[pl.ds(24 + 32 * i + dx * N_GY + dy, 32), :]
            inside = (tile_y + dy >= 0) & (tile_y + dy < N_GY) & (lane < 96)
            near = jnp.where(inside, near, 0.0)
            if d < 3:
                near = jnp.where(lane < 96, near, roll(by_owner[32 * i : 32 * i + 32], 96 - 32 * d))
            made_send[pl.ds(256 * i + d, 32, stride=8), :] = near
        part = pl.ds(256 * i, 256)
        copies.append(pltpu.make_async_copy(made_send.at[part], send.at[part], sems.at[i]))
        copies[i].start()
    for copy in copies:
        copy.wait()


def stencil_tools(main_v, main_s, strip_v, strip_s):
    lane = lanes_of((8, 128))
    last = lane == 127
    first = lane == 0

    def load(ref, p, r):
        if r < 0:
            return pltpu.roll(ref[p, 0:8, :], 1, 0)
        if r > ROWS - 8:
            return pltpu.roll(ref[p, ROWS - 8 : ROWS, :], 7, 0)
        return ref[p, r : r + 8, :]

    def mload(f, z, r):
        return load(main_v, f * NZ + z, r) if f < 3 else load(main_s, (f - 3) * NZ + z, r)

    def sload(f, side, r):
        return load(strip_v, 2 * f + side, r) if f < 3 else load(strip_s, 2 * f - 6 + side, r)

    def next_x(value, edge, z):
        return jnp.where(last, roll(edge, 127 - (16 * z + 8)), roll(value, -1))

    def prev_x(value, edge, z):
        return jnp.where(first, roll(edge, -(16 * z + 7)), roll(value, 1))

    def next_z(value):
        return jnp.where(lane < 112, roll(value, -16), 0.0)

    def prev_z(value):
        return jnp.where(lane >= 16, roll(value, 16), 0.0)

    return mload, sload, next_x, prev_x, next_z, prev_z


def stress_planes(tools, mats, main_s, kern, g, forward, update):
    mload, sload, next_x, prev_x = tools[:4]
    zero = jnp.zeros((8, 128), F32)
    r = 8 * g
    left_vx = sload(VX, 0, r)
    right_vy, right_vz = sload(VY, 1, r), sload(VZ, 1, r)
    vx, vy = mload(VX, 0, r), mload(VY, 0, r)
    below_vz = zero
    for z in range(NZ):
        vz = mload(VZ, z, r)
        above_vx = mload(VX, z + 1, r) if z < NZ - 1 else zero
        above_vy = mload(VY, z + 1, r) if z < NZ - 1 else zero
        exx = vx - prev_x(vx, left_vx, z)
        eyy = vy - mload(VY, z, r - 1)
        ezz = vz - below_vz
        dilation = exx + eyy + ezz
        exy = (mload(VX, z, r + 1) - vx) + (next_x(vy, right_vy, z) - vy)
        if forward is not None:
            for k, strain in ((0, dilation), (1, exy)):
                at = pl.ds((k * NZ + z) * CY + 8 * (g - 1), 8)
                kern[at, :] = kern[at, :] + forward(k, z) * strain
        if update:
            exz = (above_vx - vx) + (next_x(vz, right_vz, z) - vz)
            eyz = (above_vy - vy) + (mload(VZ, z, r + 1) - vz)
            pressure = mats[z, pl.ds(r, 8), :] * dilation
            hm = mats[NZ + z, pl.ds(r, 8), :]
            hm2 = hm + hm
            for f, change in (
                (SXX, pressure + hm2 * exx),
                (SYY, pressure + hm2 * eyy),
                (SZZ, pressure + hm2 * ezz),
                (SXY, hm * exy),
                (SXZ, hm * exz),
                (SYZ, hm * eyz),
            ):
                main_s[(f - 3) * NZ + z, pl.ds(r, 8), :] = mload(f, z, r) + change
        vx, vy, below_vz = above_vx, above_vy, vz


def step_kernel(
    v_in,
    s_in,
    mats,
    own_right,
    own_left,
    from_left,
    from_right,
    forward_dilation,
    forward_shear,
    sources,
    tile_map,
    main_v,
    main_s,
    send,
    strip_out,
    strip_v,
    strip_s,
    mat_strips,
    fd,
    fs,
    plane_src,
    kern,
    made_send,
    sems,
):
    del v_in, s_in
    def forward_copies(t):
        return (
            pltpu.make_async_copy(forward_dilation.at[t], fd.at[t], sems.at[t]),
            pltpu.make_async_copy(forward_shear.at[t], fs.at[t], sems.at[STEPS + t]),
        )

    for t in range(STEPS):
        for made in forward_copies(t):
            made.start()
    edges = (own_right, own_left, from_left, from_right)
    zero = jnp.zeros((8, 128), F32)
    for p in range(2 * NZ):
        for g in range(CY // 8):
            kern[pl.ds(p * CY + 8 * g, 8), :] = zero

    tile_x, tile_y = lax.axis_index("gx"), lax.axis_index("gy")
    me = tile_x * N_GY + tile_y
    lane = lanes_of((8, 128))
    row = rows_of((8, 128))

    low = lane // 8 % 2 == 0
    for pair in range(FIELDS // 2):
        for g in range(GROUPS):
            sr, sl, rl, rr = (ref[pair * GROUPS + g] for ref in edges)
            made = (
                jnp.where(low, rl, sl),
                jnp.where(low, sr, rr),
                jnp.where(low, roll(rl, -8), roll(sl, 8)),
                jnp.where(low, roll(sr, -8), roll(rr, 8)),
            )
            for i in range(4):
                at = 4 * pair + i
                if at < 6:
                    strip_v[at, 8 * g : 8 * g + 8, :] = made[i]
                elif at < 2 * WAVES:
                    strip_s[at - 6, 8 * g : 8 * g + 8, :] = made[i]
                else:
                    mat_strips[at - 2 * WAVES, 8 * g : 8 * g + 8, :] = made[i]
    def add_sender(i, carry):
        parts = [sources[pl.ds(pl.multiple_of(i * 128 + 8 * j, 8), 8), :] for j in range(16)]
        while len(parts) > 1:
            parts = [a + b for a, b in zip(parts[::2], parts[1::2])]
        return carry + parts[0]

    got = lax.fori_loop(0, OWNERS // 16, add_sender, zero)
    own = zero
    for d in range(3):
        own = jnp.where(lane // 32 == d, roll(got, 32 + 32 * d)[d : d + 1], own)
    own = jnp.where((row == 0) & (lane < 96), own, 0.0)
    full = jnp.concatenate([got, own, jnp.zeros((112, 128), F32)], 0)
    turned = jnp.transpose(full)
    values = jnp.zeros((24, 128), F32)
    lane24 = lanes_of((24, 128))
    for k in range(4):
        part = turned[k * 24 : (k + 1) * 24]
        values = jnp.where(lane24 // 16 == k, roll(part, 16 * k), values)
    high, middle, low = three_parts(values)
    high, middle, low = high.astype(F32), middle.astype(F32), low.astype(F32)
    values = jnp.concatenate([jnp.where(lane24 < 64, high, roll(middle, 64)), low], 1)

    row16 = rows_of((16, 128))
    cells = jnp.zeros((16, 128), F32)
    for d, (dx, dy) in enumerate(AROUND + [(0, 0)]):
        line = edges[(0, 3, 2)[dx]][EDGES][dy + 1 : dy + 2]
        cells = jnp.where(row16 == d, line, cells)
    turned = jnp.transpose(jnp.concatenate([cells, jnp.zeros((112, 128), F32)], 0))
    lane1 = lanes_of((1, 128))
    across = jnp.zeros((1, 128), F32)
    for k in range(4):
        across = jnp.where(lane1 // 16 == k, roll(turned[k : k + 1], 16 * k), across)
    across = jnp.where(lane1 < 64, across, roll(across, 64)).astype(jnp.int32)
    across = jnp.concatenate([across, across], 1)
    along = jnp.concatenate([jnp.broadcast_to(cells[:, k : k + 1], (16, 256)) for k in range(4)], 0)
    along = along.astype(jnp.int32)
    at_row = rows_of((ROWS, 256)) == across // NX - tile_y * CY + HALO
    at_x = along % NX - tile_x * CX
    n = lanes_of((64, 256))
    hit = (n == at_x) & (n < 128)
    hit = hit | ((n - 128 == at_x + 8) & (n >= 128) & (n < 144))
    hit = hit | ((n - 192 == at_x - 120) & (n >= 192) & (n < 208))
    hit = jnp.where(hit, 1.0, 0.0).astype(BF16)
    hit = jnp.concatenate([hit, hit, hit, hit], 0)
    spread = jnp.concatenate(
        [jnp.where(at_row, values[i : i + 1], 0.0).astype(BF16) for i in range(24)], 0
    )
    plane_src[...] = jnp.dot(spread, hit, preferred_element_type=F32)

    tools = stencil_tools(main_v, main_s, strip_v, strip_s)
    mload, sload, next_x, prev_x, next_z, prev_z = tools

    def velocity_group(step, g):
        r = 8 * g
        edges = {(f, s): sload(f, s, r) for f in range(SXX, WAVES) for s in range(2)}
        below_xz = below_yz = zero
        zz = mload(SZZ, 0, r)
        for z in range(NZ):
            xx, xy, yy, xz, yz = (mload(f, z, r) for f in (SXX, SXY, SYY, SXZ, SYZ))
            above_zz = mload(SZZ, z + 1, r) if z < NZ - 1 else zero
            ax = (next_x(xx, edges[SXX, 1], z) - xx) + (xy - mload(SXY, z, r - 1)) + (xz - below_xz)
            ay = (xy - prev_x(xy, edges[SXY, 0], z)) + (mload(SYY, z, r + 1) - yy) + (yz - below_yz)
            az = (xz - prev_x(xz, edges[SXZ, 0], z)) + (yz - mload(SYZ, z, r - 1)) + (above_zz - zz)
            below_xz, below_yz, zz = xz, yz, above_zz
            hb = mats[2 * NZ + z, pl.ds(r, 8), :]
            for c, a in enumerate((ax, ay, az)):
                if z == 0:
                    at = pl.multiple_of((c * STEPS + step) * ROWS + 8 * g, 8)
                    a = a + plane_src[pl.ds(at, 8), 0:128]
                main_v[c * NZ + z, pl.ds(r, 8), :] = mload(c, z, r) + hb * a
        for side in range(2):
            xx, yy, zz, xy, xz, yz = (edges[f, side] for f in (SXX, SYY, SZZ, SXY, SXZ, SYZ))
            ax = (roll(xx, -1) - xx) + (xy - sload(SXY, side, r - 1)) + (xz - prev_z(xz))
            ay = (xy - roll(xy, 1)) + (sload(SYY, side, r + 1) - yy) + (yz - prev_z(yz))
            az = (xz - roll(xz, 1)) + (yz - sload(SYZ, side, r - 1)) + (next_z(zz) - zz)
            hb = mat_strips[2 * 2 + side, pl.ds(r, 8), :]
            for c, a in enumerate((ax, ay, az)):
                at = pl.multiple_of((c * STEPS + step) * ROWS + 8 * g, 8)
                src = plane_src[pl.ds(at, 8), 128:256]
                src = jnp.where(lane < 16, roll(src, 64) if side else src, 0.0)
                strip_v[2 * c + side, pl.ds(r, 8), :] = sload(c, side, r) + hb * (a + src)

    def stress_strips(g):
        r = 8 * g
        for side in range(2):
            vx, vy, vz = (sload(f, side, r) for f in range(3))
            exx = vx - roll(vx, 1)
            eyy = vy - sload(VY, side, r - 1)
            ezz = vz - prev_z(vz)
            exy = (sload(VX, side, r + 1) - vx) + (roll(vy, -1) - vy)
            exz = (next_z(vx) - vx) + (roll(vz, -1) - vz)
            eyz = (next_z(vy) - vy) + (sload(VZ, side, r + 1) - vz)
            pressure = mat_strips[side, pl.ds(r, 8), :] * (exx + eyy + ezz)
            hm = mat_strips[2 + side, pl.ds(r, 8), :]
            hm2 = hm + hm
            for f, change in (
                (SXX, pressure + hm2 * exx),
                (SYY, pressure + hm2 * eyy),
                (SZZ, pressure + hm2 * ezz),
                (SXY, hm * exy),
                (SXZ, hm * exz),
                (SYZ, hm * eyz),
            ):
                strip_s[2 * f - 6 + side, pl.ds(r, 8), :] = sload(f, side, r) + change

    def stress_rows(step, g, update):
        forward = None
        if 0 < g < GROUPS - 1:
            at = (g - 1) // 2 * 16

            def forward(k, z):
                both = (fd, fs)[k][step, z, at : at + 16, :].astype(F32)
                return both[(g - 1) % 2 * 8 : (g - 1) % 2 * 8 + 8]

        if update or forward is not None:
            stress_planes(tools, mats, main_s, kern, g, forward, update)
        if update:
            stress_strips(g)

    def step_rows(step, update):
        for made in forward_copies(step):
            made.wait()
        for g in range(GROUPS):
            velocity_group(step, g)
            if g > 0:
                stress_rows(step, g - 1, update)
        stress_rows(step, GROUPS - 1, update)

    def one_step(step, carry):
        step_rows(step, True)
        return carry

    lax.fori_loop(0, STEPS - 1, one_step, 0)
    step_rows(STEPS - 1, False)
    strip_copy = pltpu.make_async_copy(strip_v, strip_out, sems.at[2 * STEPS])
    strip_copy.start()

    slot = tile_map[...] // 256 * 2 + (tile_map[...] % 256 - 2 * me)
    slot = slot.astype(F32)
    line = jnp.zeros((8, 128), F32)
    for y in range(8):
        half = slot[:, 128 * (y // 4) : 128 * (y // 4) + 128]
        line = jnp.where(row == y, roll(half, -32 * (y % 4)), line)
    widen = jnp.where(lanes_of((128, 128)) // 4 == rows_of((128, 128)), 1.0, 0.0).astype(BF16)
    line = jnp.where(lane < 32, line, 0.0).astype(BF16)
    line = jnp.dot(line, widen, preferred_element_type=F32)
    place = rows_of((256, 128)).astype(F32)
    put = jnp.concatenate(
        [jnp.where(line[y : y + 1] == place, H / 16, 0.0).astype(BF16) for y in range(8)], 1
    )
    sums = []
    for y in range(8):
        parts = [kern[pl.ds(4 * y + i, 2 * NZ, stride=CY), :] for i in range(4)]
        sums.append((parts[0] + parts[1]) + (parts[2] + parts[3]))
    sums = jnp.concatenate(three_parts(jnp.concatenate(sums, 1)), 0)
    placed = lax.dot_general(put, sums, (((1,), (1,)), ((), ())), preferred_element_type=F32)
    placed = placed[:, 0:16] + placed[:, 16:32] + placed[:, 32:48]
    made_send[...] = jnp.concatenate([placed, jnp.zeros((256, 112), F32)], 1)
    send_copy = pltpu.make_async_copy(made_send, send, sems.at[0])
    send_copy.start()
    send_copy.wait()
    strip_copy.wait()


def finish_kernel(velocity, s_in, mats, strip_in, stress, out, strip_v, sems):
    del s_in
    pltpu.sync_copy(strip_in, strip_v)
    tools = stencil_tools(velocity, stress, strip_v, None)
    copies = []

    def deliver(f, rows, start):
        ref, p = at_plane(velocity, stress, None, f)
        made = pltpu.make_async_copy(
            ref.at[pl.ds(p, NZ), pl.ds(HALO + start, rows), :],
            out.at[f, :, pl.ds(start, rows), :],
            sems.at[len(copies)],
        )
        made.start()
        copies.append(made)

    for f in range(3):
        deliver(f, CY, 0)
    for g in range(CY // 8):
        stress_planes(tools, mats, stress, None, g + 1, None, True)
        for f in range(3, WAVES):
            deliver(f, 8, 8 * g)
    for made in copies:
        made.wait()


def turn_kernel(got, out):
    out[...] = jnp.transpose(got[...])[0:16]


def shift(value, dx, dy):
    pairs = [
        (x * N_GY + y, (x + dx) * N_GY + y + dy)
        for x in range(N_GX)
        for y in range(N_GY)
        if 0 <= x + dx < N_GX and 0 <= y + dy < N_GY
    ]
    return lax.ppermute(value, ("gx", "gy"), pairs)


def shape(*dims):
    return jax.ShapeDtypeStruct(dims, F32)


def cost(flops, data):
    return pl.CostEstimate(flops=flops, bytes_accessed=data, transcendentals=0)


def local(
    adjoint_state,
    lame_lambda,
    shear_modulus,
    buoyancy,
    forward_dilation,
    forward_shear,
    residual,
    sample_counts,
    station_list,
    receiver_cells,
    tile_map,
):
    rows_dev = residual.shape[0]
    in_hbm = lambda value: pltpu.with_memory_space_constraint(value, pltpu.HBM)
    adjoint_state, lame_lambda, shear_modulus, buoyancy, forward_dilation, forward_shear = (
        in_hbm(value)
        for value in (
            adjoint_state,
            lame_lambda,
            shear_modulus,
            buoyancy,
            forward_dilation,
            forward_shear,
        )
    )

    held = (shape(3 * NZ, ROWS, 128), shape(6 * NZ, ROWS, 128), shape(3 * NZ, ROWS, 128))
    velocity, stress, mats, up, down, by_owner = pl.pallas_call(
        first_kernel,
        out_shape=held + (shape(PLANES + 1, 8, 128), shape(PLANES + 1, 8, 128), shape(128, 128)),
        in_specs=[ANY] * 4 + [SMEM, ANY, VMEM, VMEM, ANY],
        out_specs=(VMEM,) * 6,
        scratch_shapes=[
            pltpu.VMEM((SAMPLES // STEPS, 128), BF16),
            pltpu.VMEM((SAMPLES, 128), BF16),
            pltpu.VMEM((3, rows_dev, SAMPLES), BF16),
            pltpu.SemaphoreType.DMA((FIELDS + 4,)),
        ],
        compiler_params=PART,
        cost_estimate=cost(1 << 30, 1 << 22),
    )(
        adjoint_state,
        lame_lambda,
        shear_modulus,
        buoyancy,
        in_hbm(receiver_cells.reshape(1, 4)),
        in_hbm(jnp.transpose(residual, (1, 0, 2))),
        in_hbm(sample_counts.reshape(1, rows_dev)),
        in_hbm(station_list.reshape(1, rows_dev)),
        in_hbm(jnp.asarray(resample_table())),
    )
    from_below = shift(up, 0, 1)
    from_above = shift(down, 0, -1)

    send = pl.pallas_call(
        send_kernel,
        out_shape=pltpu.HBM((OWNERS * 8, 128), F32),
        in_specs=[VMEM],
        out_specs=ANY,
        scratch_shapes=[
            pltpu.VMEM((OWNERS * 8, 128), F32),
            pltpu.VMEM((176, 128), F32),
            pltpu.SemaphoreType.DMA((4,)),
        ],
        compiler_params=PART,
        cost_estimate=cost(1 << 20, 1 << 20),
    )(by_owner)
    sources = lax.all_to_all(send, ("gx", "gy"), 0, 0, tiled=True)

    velocity, stress, mats, right, left = pl.pallas_call(
        edges_kernel,
        out_shape=held + (shape(EDGES + 1, 8, 128), shape(EDGES + 1, 8, 128)),
        in_specs=[VMEM] * 6,
        out_specs=(VMEM,) * 5,
        input_output_aliases={0: 0, 1: 1, 2: 2},
        compiler_params=PART,
        cost_estimate=cost(1 << 20, 1 << 21),
    )(velocity, stress, mats, from_below, from_above, up)
    from_left = shift(right, 1, 0)
    from_right = shift(left, -1, 0)

    velocity, stress, send, strip_v = pl.pallas_call(
        step_kernel,
        out_shape=held[:2] + (pltpu.HBM((256, 128), F32), pltpu.HBM((6, ROWS, 128), F32)),
        in_specs=[VMEM] * 7 + [ANY] * 2 + [VMEM] * 2,
        out_specs=(VMEM, VMEM, ANY, ANY),
        input_output_aliases={0: 0, 1: 1},
        scratch_shapes=[
            pltpu.VMEM((6, ROWS, 128), F32),
            pltpu.VMEM((12, ROWS, 128), F32),
            pltpu.VMEM((6, ROWS, 128), F32),
            pltpu.VMEM((STEPS, NZ, CY, CX), BF16),
            pltpu.VMEM((STEPS, NZ, CY, CX), BF16),
            pltpu.VMEM((24 * ROWS, 256), F32),
            pltpu.VMEM((2 * NZ * CY, 128), F32),
            pltpu.VMEM((256, 128), F32),
            pltpu.SemaphoreType.DMA((2 * STEPS + 1,)),
        ],
        compiler_params=PART,
        cost_estimate=cost(1 << 27, 1 << 23),
    )(
        velocity,
        stress,
        mats,
        right,
        left,
        from_left,
        from_right,
        forward_dilation,
        forward_shear,
        sources,
        in_hbm(tile_map.reshape(1, 256)),
    )
    got = lax.all_to_all(send, ("gx", "gy"), 0, 0, tiled=True)
    _, adjoint_out = pl.pallas_call(
        finish_kernel,
        out_shape=(held[1], shape(WAVES, NZ, CY, CX)),
        in_specs=[VMEM] * 3 + [ANY],
        out_specs=(VMEM, ANY),
        input_output_aliases={1: 0},
        scratch_shapes=[pltpu.VMEM((6, ROWS, 128), F32), pltpu.SemaphoreType.DMA((27,))],
        compiler_params=PART,
        cost_estimate=cost(1 << 24, 1 << 22),
    )(velocity, stress, mats, strip_v)
    kernels = pl.pallas_call(
        turn_kernel,
        out_shape=shape(16, 256),
        in_specs=[VMEM],
        out_specs=VMEM,
        compiler_params=PART,
    )(got)
    return kernels.reshape(2, NZ, 256), adjoint_out


def solution(mesh):
    in_specs = (
        P(None, None, "gy", "gx"),
        P(None, "gy", "gx"),
        P(None, "gy", "gx"),
        P(None, "gy", "gx"),
        P(None, None, "gy", "gx"),
        P(None, None, "gy", "gx"),
        P(("gx", "gy"), None, None),
        P(("gx", "gy")),
        P(("gx", "gy")),
        P(("gx", "gy")),
        P(("gx", "gy")),
    )
    out_specs = (P(None, None, ("gx", "gy")), P(None, None, "gy", "gx"))
    return jax.shard_map(local, mesh=mesh, in_specs=in_specs, out_specs=out_specs, check_vma=False)
```

```python
import math

import jax
import jax.numpy as jnp
import numpy as np
from jax import lax
from jax.experimental import pallas as pl
from jax.experimental.pallas import tpu as pltpu
from jax.sharding import PartitionSpec as P

F32 = jnp.float32
BF16 = jnp.bfloat16

NZ, CY, CX = 8, 32, 128
STEPS = 8
SAMPLES = 4096
H = 0.25
N_GX, N_GY = 8, 16
OWNERS = N_GX * N_GY
NX = N_GX * CX
HALO = 8
ROWS = CY + 2 * HALO
GROUPS = ROWS // 8
FIELDS = 12
WAVES = 9
PLANES = FIELDS * NZ
EDGES = FIELDS // 2 * GROUPS

AROUND = [(dx, dy) for dx in (-1, 0, 1) for dy in (-1, 0, 1) if (dx, dy) != (0, 0)]

VX, VY, VZ, SXX, SYY, SZZ, SXY, SXZ, SYZ = range(WAVES)

VMEM = pl.BlockSpec(memory_space=pltpu.VMEM)
SMEM = pl.BlockSpec(memory_space=pltpu.SMEM)
ANY = pl.BlockSpec(memory_space=pltpu.HBM)


PART = pltpu.CompilerParams(vmem_limit_bytes=24 << 20)


def lanes_of(shape):
    return lax.broadcasted_iota(jnp.int32, shape, len(shape) - 1)


def rows_of(shape):
    return lax.broadcasted_iota(jnp.int32, shape, len(shape) - 2)


def roll(value, shift):
    return pltpu.roll(value, shift % value.shape[-1], value.ndim - 1)


def three_parts(value):
    high = value.astype(BF16)
    rest = value - high.astype(F32)
    middle = rest.astype(BF16)
    low = (rest - middle.astype(F32)).astype(BF16)
    return high, middle, low


def resample_table():
    per_step = SAMPLES // STEPS
    position = np.arange(SAMPLES, dtype=np.float32) + np.float32(0.5)
    centers = (np.arange(STEPS, dtype=np.float32) + np.float32(0.5)) * np.float32(per_step)
    distance = np.abs(position[:, None] - centers[None, :]) / np.float32(per_step)
    weight = np.maximum(np.float32(0.0), np.float32(1.0) - distance)
    table = (weight / np.float32(math.sqrt(per_step))).astype(BF16)
    wide = np.zeros((per_step, 128), BF16)
    wide[:, :96] = np.tile(table[per_step : 2 * per_step], (1, 12))
    return wide


def at_plane(velocity, stress, mats, f):
    if f < 3:
        return velocity, f * NZ
    if f < WAVES:
        return stress, (f - 3) * NZ
    return mats, (f - WAVES) * NZ


def first_kernel(
    state,
    lame,
    shear,
    buoyancy,
    cells,
    residual,
    counts,
    stations,
    weights,
    velocity,
    stress,
    mats,
    up,
    down,
    send,
    by_owner,
    made_send,
    totals,
    send_sems,
    base,
    table,
    held,
    sems,
):
    weights_in = pltpu.make_async_copy(weights, base, sems.at[FIELDS])
    weights_in.start()
    copies = []
    for f in range(FIELDS):
        to, p = at_plane(velocity, stress, mats, f)
        source = state.at[f] if f < WAVES else (lame, shear, buoyancy)[f - WAVES]
        to = to.at[pl.ds(p, NZ), pl.ds(HALO, CY), :]
        copies.append(pltpu.make_async_copy(source, to, sems.at[f]))
        copies[f].start()
    rows_in = [
        pltpu.make_async_copy(residual.at[c], held.at[c], sems.at[FIELDS + 1 + c]) for c in range(3)
    ]
    for copy in rows_in:
        copy.start()
    lane = lanes_of((8, 128))
    mine = jnp.zeros((8, 128), jnp.int32)
    for k in range(4):
        mine = jnp.where(lane == k, cells[0, k], mine)
    up[PLANES] = mine.astype(F32)
    down[PLANES] = mine.astype(F32)
    rows = held.shape[1]
    pad = jnp.zeros((1, 128 - rows), F32)
    count = column_of(jnp.concatenate([counts[...].astype(F32), pad], 1))[:rows]
    station_row = jnp.concatenate([stations[...], jnp.full((1, 128 - rows), -1, jnp.int32)], 1)
    station = column_of(station_row.astype(F32))[:rows].astype(jnp.int32)
    weights_in.wait()
    per_step = SAMPLES // STEPS
    middle = base[...].astype(F32)
    slot = lanes_of((per_step, 128)) % STEPS
    for j in range(STEPS):
        moved = roll(middle, j - 1)
        if j in (0, STEPS - 1):
            moved = jnp.where(slot == STEPS - 1 - j, 0.0, moved)
        table[per_step * j : per_step * (j + 1), :] = moved.astype(BF16)
    for f in range(FIELDS):
        copies[f].wait()
        ref, p = at_plane(velocity, stress, mats, f)
        for z in range(NZ):
            down[f * NZ + z] = ref[p + z, 8:16, :]
            up[f * NZ + z] = ref[p + z, 32:40, :]
    by_owner[...] = sums_by_owner(rows_in, held, table, count, station, station_row)
    send_kernel(by_owner, send, made_send, totals, send_sems)


def edges_kernel(v_in, s_in, m_in, below, above, own, velocity, stress, mats, right, left):
    del v_in, s_in, m_in
    lane = lanes_of((8, 128))
    for f in range(FIELDS):
        ref, p = at_plane(velocity, stress, mats, f)
        for z in range(NZ):
            if f < WAVES:
                ref[p + z, 0:8, :] = below[f * NZ + z]
                ref[p + z, 40:48, :] = above[f * NZ + z]
            else:
                ref[p + z, 0:8, :] = H * below[f * NZ + z]
                ref[p + z, 8:40, :] = H * ref[p + z, 8:40, :]
                ref[p + z, 40:48, :] = H * above[f * NZ + z]
    for group in range(GROUPS):
        tails, heads = [], []
        for f in range(FIELDS):
            ref, p = at_plane(velocity, stress, mats, f)
            tail = jnp.zeros((8, 128), F32)
            head = jnp.zeros((8, 128), F32)
            for z in range(NZ):
                plane = ref[p + z, 8 * group : 8 * group + 8, :]
                tail = jnp.where(lane // 8 == 2 * z, roll(plane, 16 * z - 120), tail)
                head = jnp.where(lane // 8 == 2 * z + 1, roll(plane, 16 * z + 8), head)
            tails.append(tail)
            heads.append(head)
        for pair in range(FIELDS // 2):
            right[pair * GROUPS + group] = tails[2 * pair] + roll(tails[2 * pair + 1], 8)
            left[pair * GROUPS + group] = heads[2 * pair] + roll(heads[2 * pair + 1], -8)
    row = rows_of((8, 128))
    cells = jnp.where(row == 0, below[PLANES], jnp.where(row == 1, own[PLANES], above[PLANES]))
    right[EDGES] = cells
    left[EDGES] = cells


def column_of(row_vector):
    return jnp.transpose(jnp.broadcast_to(row_vector, (128, 128)))


def sums_by_owner(rows_in, held, table, count, station, station_row):
    rows = held.shape[1]
    lane = lanes_of((rows, 128))
    total = jnp.zeros((rows, 128), F32)
    live = jnp.concatenate(
        [
            jnp.where((lane + 128 * g).astype(F32) < count, 1.0, 0.0).astype(BF16)
            for g in range(SAMPLES // 128)
        ],
        1,
    )
    for c in range(3):
        rows_in[c].wait()
        product = jnp.dot(held[c] * live, table[...], preferred_element_type=F32)
        total = jnp.where(lane // 8 % 3 == c, product, total)
    mine = jnp.where(lane // 24 == station % 4, total, 0.0)
    mine = jnp.concatenate([mine, jnp.zeros((128 - rows, 128), F32)], 0)
    names = jnp.where(rows_of((128, 128)) == station_row // 4, 1.0, 0.0)
    return jnp.dot(names, mine, preferred_element_type=F32, precision=lax.Precision.HIGHEST)


def send_kernel(by_owner, send, made_send, totals, sems):
    totals[0:24, :] = jnp.zeros((24, 128), F32)
    totals[152:176, :] = jnp.zeros((24, 128), F32)
    totals[24:152, :] = by_owner[...]
    lane = lanes_of((32, 128))
    tile_y = rows_of((32, 128)) % N_GY
    copies = []
    for i in range(OWNERS // 32):
        for d, (dx, dy) in enumerate(AROUND):
            near = totals[pl.ds(24 + 32 * i + dx * N_GY + dy, 32), :]
            inside = (tile_y + dy >= 0) & (tile_y + dy < N_GY) & (lane < 96)
            near = jnp.where(inside, near, 0.0)
            if d < 3:
                near = jnp.where(lane < 96, near, roll(by_owner[32 * i : 32 * i + 32], 96 - 32 * d))
            made_send[pl.ds(256 * i + d, 32, stride=8), :] = near
        part = pl.ds(256 * i, 256)
        copies.append(pltpu.make_async_copy(made_send.at[part], send.at[part], sems.at[i]))
        copies[i].start()
    for copy in copies:
        copy.wait()


def stencil_tools(main_v, main_s, strip_v, strip_s):
    lane = lanes_of((8, 128))
    last = lane == 127
    first = lane == 0

    def load(ref, p, r):
        if r < 0:
            return pltpu.roll(ref[p, 0:8, :], 1, 0)
        if r > ROWS - 8:
            return pltpu.roll(ref[p, ROWS - 8 : ROWS, :], 7, 0)
        return ref[p, r : r + 8, :]

    def mload(f, z, r):
        return load(main_v, f * NZ + z, r) if f < 3 else load(main_s, (f - 3) * NZ + z, r)

    def sload(f, side, r):
        return load(strip_v, 2 * f + side, r) if f < 3 else load(strip_s, 2 * f - 6 + side, r)

    def next_x(value, edge, z):
        return jnp.where(last, roll(edge, 127 - (16 * z + 8)), roll(value, -1))

    def prev_x(value, edge, z):
        return jnp.where(first, roll(edge, -(16 * z + 7)), roll(value, 1))

    def next_z(value):
        return jnp.where(lane < 112, roll(value, -16), 0.0)

    def prev_z(value):
        return jnp.where(lane >= 16, roll(value, 16), 0.0)

    return mload, sload, next_x, prev_x, next_z, prev_z


def stress_planes(tools, mats, main_s, kern, g, forward, update):
    mload, sload, next_x, prev_x = tools[:4]
    zero = jnp.zeros((8, 128), F32)
    r = 8 * g
    left_vx = sload(VX, 0, r)
    right_vy, right_vz = sload(VY, 1, r), sload(VZ, 1, r)
    vx, vy = mload(VX, 0, r), mload(VY, 0, r)
    below_vz = zero
    for z in range(NZ):
        vz = mload(VZ, z, r)
        above_vx = mload(VX, z + 1, r) if z < NZ - 1 else zero
        above_vy = mload(VY, z + 1, r) if z < NZ - 1 else zero
        exx = vx - prev_x(vx, left_vx, z)
        eyy = vy - mload(VY, z, r - 1)
        ezz = vz - below_vz
        dilation = exx + eyy + ezz
        exy = (mload(VX, z, r + 1) - vx) + (next_x(vy, right_vy, z) - vy)
        if forward is not None:
            for k, strain in ((0, dilation), (1, exy)):
                at = pl.ds((k * NZ + z) * CY + 8 * (g - 1), 8)
                kern[at, :] = kern[at, :] + forward(k, z) * strain
        if update:
            exz = (above_vx - vx) + (next_x(vz, right_vz, z) - vz)
            eyz = (above_vy - vy) + (mload(VZ, z, r + 1) - vz)
            pressure = mats[z, pl.ds(r, 8), :] * dilation
            hm = mats[NZ + z, pl.ds(r, 8), :]
            hm2 = hm + hm
            for f, change in (
                (SXX, pressure + hm2 * exx),
                (SYY, pressure + hm2 * eyy),
                (SZZ, pressure + hm2 * ezz),
                (SXY, hm * exy),
                (SXZ, hm * exz),
                (SYZ, hm * eyz),
            ):
                main_s[(f - 3) * NZ + z, pl.ds(r, 8), :] = mload(f, z, r) + change
        vx, vy, below_vz = above_vx, above_vy, vz


def step_kernel(
    v_in,
    s_in,
    mats,
    own_right,
    own_left,
    from_left,
    from_right,
    forward_dilation,
    forward_shear,
    sources,
    tile_map,
    main_v,
    main_s,
    send,
    strip_out,
    strip_v,
    strip_s,
    mat_strips,
    fd,
    fs,
    plane_src,
    kern,
    made_send,
    sems,
):
    del v_in, s_in
    def forward_copies(t):
        return (
            pltpu.make_async_copy(forward_dilation.at[t], fd.at[t], sems.at[t]),
            pltpu.make_async_copy(forward_shear.at[t], fs.at[t], sems.at[STEPS + t]),
        )

    for t in range(STEPS):
        for made in forward_copies(t):
            made.start()
    edges = (own_right, own_left, from_left, from_right)
    zero = jnp.zeros((8, 128), F32)
    for p in range(2 * NZ):
        for g in range(CY // 8):
            kern[pl.ds(p * CY + 8 * g, 8), :] = zero

    tile_x, tile_y = lax.axis_index("gx"), lax.axis_index("gy")
    me = tile_x * N_GY + tile_y
    lane = lanes_of((8, 128))
    row = rows_of((8, 128))

    low = lane // 8 % 2 == 0
    for pair in range(FIELDS // 2):
        for g in range(GROUPS):
            sr, sl, rl, rr = (ref[pair * GROUPS + g] for ref in edges)
            made = (
                jnp.where(low, rl, sl),
                jnp.where(low, sr, rr),
                jnp.where(low, roll(rl, -8), roll(sl, 8)),
                jnp.where(low, roll(sr, -8), roll(rr, 8)),
            )
            for i in range(4):
                at = 4 * pair + i
                if at < 6:
                    strip_v[at, 8 * g : 8 * g + 8, :] = made[i]
                elif at < 2 * WAVES:
                    strip_s[at - 6, 8 * g : 8 * g + 8, :] = made[i]
                else:
                    mat_strips[at - 2 * WAVES, 8 * g : 8 * g + 8, :] = made[i]
    def add_sender(i, carry):
        parts = [sources[pl.ds(pl.multiple_of(i * 128 + 8 * j, 8), 8), :] for j in range(16)]
        while len(parts) > 1:
            parts = [a + b for a, b in zip(parts[::2], parts[1::2])]
        return carry + parts[0]

    got = lax.fori_loop(0, OWNERS // 16, add_sender, zero)
    own = zero
    for d in range(3):
        own = jnp.where(lane // 32 == d, roll(got, 32 + 32 * d)[d : d + 1], own)
    own = jnp.where((row == 0) & (lane < 96), own, 0.0)
    full = jnp.concatenate([got, own, jnp.zeros((112, 128), F32)], 0)
    turned = jnp.transpose(full)
    values = jnp.zeros((24, 128), F32)
    lane24 = lanes_of((24, 128))
    for k in range(4):
        part = turned[k * 24 : (k + 1) * 24]
        values = jnp.where(lane24 // 16 == k, roll(part, 16 * k), values)
    high, middle, low = three_parts(values)
    high, middle, low = high.astype(F32), middle.astype(F32), low.astype(F32)
    values = jnp.concatenate([jnp.where(lane24 < 64, high, roll(middle, 64)), low], 1)

    row16 = rows_of((16, 128))
    cells = jnp.zeros((16, 128), F32)
    for d, (dx, dy) in enumerate(AROUND + [(0, 0)]):
        line = edges[(0, 3, 2)[dx]][EDGES][dy + 1 : dy + 2]
        cells = jnp.where(row16 == d, line, cells)
    turned = jnp.transpose(jnp.concatenate([cells, jnp.zeros((112, 128), F32)], 0))
    lane1 = lanes_of((1, 128))
    across = jnp.zeros((1, 128), F32)
    for k in range(4):
        across = jnp.where(lane1 // 16 == k, roll(turned[k : k + 1], 16 * k), across)
    across = jnp.where(lane1 < 64, across, roll(across, 64)).astype(jnp.int32)
    across = jnp.concatenate([across, across], 1)
    along = jnp.concatenate([jnp.broadcast_to(cells[:, k : k + 1], (16, 256)) for k in range(4)], 0)
    along = along.astype(jnp.int32)
    at_row = rows_of((ROWS, 256)) == across // NX - tile_y * CY + HALO
    at_x = along % NX - tile_x * CX
    n = lanes_of((64, 256))
    hit = (n == at_x) & (n < 128)
    hit = hit | ((n - 128 == at_x + 8) & (n >= 128) & (n < 144))
    hit = hit | ((n - 192 == at_x - 120) & (n >= 192) & (n < 208))
    hit = jnp.where(hit, 1.0, 0.0).astype(BF16)
    hit = jnp.concatenate([hit, hit, hit, hit], 0)
    spread = jnp.concatenate(
        [jnp.where(at_row, values[i : i + 1], 0.0).astype(BF16) for i in range(24)], 0
    )
    plane_src[...] = jnp.dot(spread, hit, preferred_element_type=F32)

    tools = stencil_tools(main_v, main_s, strip_v, strip_s)
    mload, sload, next_x, prev_x, next_z, prev_z = tools

    def velocity_group(step, g):
        r = 8 * g
        edges = {(f, s): sload(f, s, r) for f in range(SXX, WAVES) for s in range(2)}
        below_xz = below_yz = zero
        zz = mload(SZZ, 0, r)
        for z in range(NZ):
            xx, xy, yy, xz, yz = (mload(f, z, r) for f in (SXX, SXY, SYY, SXZ, SYZ))
            above_zz = mload(SZZ, z + 1, r) if z < NZ - 1 else zero
            ax = (next_x(xx, edges[SXX, 1], z) - xx) + (xy - mload(SXY, z, r - 1)) + (xz - below_xz)
            ay = (xy - prev_x(xy, edges[SXY, 0], z)) + (mload(SYY, z, r + 1) - yy) + (yz - below_yz)
            az = (xz - prev_x(xz, edges[SXZ, 0], z)) + (yz - mload(SYZ, z, r - 1)) + (above_zz - zz)
            below_xz, below_yz, zz = xz, yz, above_zz
            hb = mats[2 * NZ + z, pl.ds(r, 8), :]
            for c, a in enumerate((ax, ay, az)):
                if z == 0:
                    at = pl.multiple_of((c * STEPS + step) * ROWS + 8 * g, 8)
                    a = a + plane_src[pl.ds(at, 8), 0:128]
                main_v[c * NZ + z, pl.ds(r, 8), :] = mload(c, z, r) + hb * a
        for side in range(2):
            xx, yy, zz, xy, xz, yz = (edges[f, side] for f in (SXX, SYY, SZZ, SXY, SXZ, SYZ))
            ax = (roll(xx, -1) - xx) + (xy - sload(SXY, side, r - 1)) + (xz - prev_z(xz))
            ay = (xy - roll(xy, 1)) + (sload(SYY, side, r + 1) - yy) + (yz - prev_z(yz))
            az = (xz - roll(xz, 1)) + (yz - sload(SYZ, side, r - 1)) + (next_z(zz) - zz)
            hb = mat_strips[2 * 2 + side, pl.ds(r, 8), :]
            for c, a in enumerate((ax, ay, az)):
                at = pl.multiple_of((c * STEPS + step) * ROWS + 8 * g, 8)
                src = plane_src[pl.ds(at, 8), 128:256]
                src = jnp.where(lane < 16, roll(src, 64) if side else src, 0.0)
                strip_v[2 * c + side, pl.ds(r, 8), :] = sload(c, side, r) + hb * (a + src)

    def stress_strips(g):
        r = 8 * g
        for side in range(2):
            vx, vy, vz = (sload(f, side, r) for f in range(3))
            exx = vx - roll(vx, 1)
            eyy = vy - sload(VY, side, r - 1)
            ezz = vz - prev_z(vz)
            exy = (sload(VX, side, r + 1) - vx) + (roll(vy, -1) - vy)
            exz = (next_z(vx) - vx) + (roll(vz, -1) - vz)
            eyz = (next_z(vy) - vy) + (sload(VZ, side, r + 1) - vz)
            pressure = mat_strips[side, pl.ds(r, 8), :] * (exx + eyy + ezz)
            hm = mat_strips[2 + side, pl.ds(r, 8), :]
            hm2 = hm + hm
            for f, change in (
                (SXX, pressure + hm2 * exx),
                (SYY, pressure + hm2 * eyy),
                (SZZ, pressure + hm2 * ezz),
                (SXY, hm * exy),
                (SXZ, hm * exz),
                (SYZ, hm * eyz),
            ):
                strip_s[2 * f - 6 + side, pl.ds(r, 8), :] = sload(f, side, r) + change

    def stress_rows(step, g, update):
        forward = None
        if 0 < g < GROUPS - 1:
            at = (g - 1) // 2 * 16

            def forward(k, z):
                both = (fd, fs)[k][step, z, at : at + 16, :].astype(F32)
                return both[(g - 1) % 2 * 8 : (g - 1) % 2 * 8 + 8]

        if update or forward is not None:
            stress_planes(tools, mats, main_s, kern, g, forward, update)
        if update:
            stress_strips(g)

    def step_rows(step, update):
        for made in forward_copies(step):
            made.wait()
        for g in range(GROUPS):
            velocity_group(step, g)
            if g > 0:
                stress_rows(step, g - 1, update)
        stress_rows(step, GROUPS - 1, update)

    def one_step(step, carry):
        step_rows(step, True)
        return carry

    lax.fori_loop(0, STEPS - 1, one_step, 0)
    step_rows(STEPS - 1, False)
    strip_copy = pltpu.make_async_copy(strip_v, strip_out, sems.at[2 * STEPS])
    strip_copy.start()

    slot = tile_map[...] // 256 * 2 + (tile_map[...] % 256 - 2 * me)
    slot = slot.astype(F32)
    line = jnp.zeros((8, 128), F32)
    for y in range(8):
        half = slot[:, 128 * (y // 4) : 128 * (y // 4) + 128]
        line = jnp.where(row == y, roll(half, -32 * (y % 4)), line)
    widen = jnp.where(lanes_of((128, 128)) // 4 == rows_of((128, 128)), 1.0, 0.0).astype(BF16)
    line = jnp.where(lane < 32, line, 0.0).astype(BF16)
    line = jnp.dot(line, widen, preferred_element_type=F32)
    place = rows_of((256, 128)).astype(F32)
    put = jnp.concatenate(
        [jnp.where(line[y : y + 1] == place, H / 16, 0.0).astype(BF16) for y in range(8)], 1
    )
    sums = []
    for y in range(8):
        parts = [kern[pl.ds(4 * y + i, 2 * NZ, stride=CY), :] for i in range(4)]
        sums.append((parts[0] + parts[1]) + (parts[2] + parts[3]))
    sums = jnp.concatenate(three_parts(jnp.concatenate(sums, 1)), 0)
    placed = lax.dot_general(put, sums, (((1,), (1,)), ((), ())), preferred_element_type=F32)
    placed = placed[:, 0:16] + placed[:, 16:32] + placed[:, 32:48]
    made_send[...] = jnp.concatenate([placed, jnp.zeros((256, 112), F32)], 1)
    send_copy = pltpu.make_async_copy(made_send, send, sems.at[0])
    send_copy.start()
    send_copy.wait()
    strip_copy.wait()


def finish_kernel(velocity, s_in, mats, strip_in, stress, out, strip_v, sems):
    del s_in
    pltpu.sync_copy(strip_in, strip_v)
    tools = stencil_tools(velocity, stress, strip_v, None)
    copies = []

    def deliver(f, rows, start):
        ref, p = at_plane(velocity, stress, None, f)
        made = pltpu.make_async_copy(
            ref.at[pl.ds(p, NZ), pl.ds(HALO + start, rows), :],
            out.at[f, :, pl.ds(start, rows), :],
            sems.at[len(copies)],
        )
        made.start()
        copies.append(made)

    for f in range(3):
        deliver(f, CY, 0)
    for g in range(CY // 8):
        stress_planes(tools, mats, stress, None, g + 1, None, True)
        for f in range(3, WAVES):
            deliver(f, 8, 8 * g)
    for made in copies:
        made.wait()


def turn_kernel(got, out):
    out[...] = jnp.transpose(got[...])[0:16]


def shift(value, dx, dy):
    pairs = [
        (x * N_GY + y, (x + dx) * N_GY + y + dy)
        for x in range(N_GX)
        for y in range(N_GY)
        if 0 <= x + dx < N_GX and 0 <= y + dy < N_GY
    ]
    return lax.ppermute(value, ("gx", "gy"), pairs)


def shape(*dims):
    return jax.ShapeDtypeStruct(dims, F32)


def cost(flops, data):
    return pl.CostEstimate(flops=flops, bytes_accessed=data, transcendentals=0)


def local(
    adjoint_state,
    lame_lambda,
    shear_modulus,
    buoyancy,
    forward_dilation,
    forward_shear,
    residual,
    sample_counts,
    station_list,
    receiver_cells,
    tile_map,
):
    rows_dev = residual.shape[0]
    in_hbm = lambda value: pltpu.with_memory_space_constraint(value, pltpu.HBM)
    adjoint_state, lame_lambda, shear_modulus, buoyancy, forward_dilation, forward_shear = (
        in_hbm(value)
        for value in (
            adjoint_state,
            lame_lambda,
            shear_modulus,
            buoyancy,
            forward_dilation,
            forward_shear,
        )
    )

    held = (shape(3 * NZ, ROWS, 128), shape(6 * NZ, ROWS, 128), shape(3 * NZ, ROWS, 128))
    velocity, stress, mats, up, down, send = pl.pallas_call(
        first_kernel,
        out_shape=held + (shape(PLANES + 1, 8, 128), shape(PLANES + 1, 8, 128), pltpu.HBM((OWNERS * 8, 128), F32)),
        in_specs=[ANY] * 4 + [SMEM, ANY, VMEM, VMEM, ANY],
        out_specs=(VMEM,) * 5 + (ANY,),
        scratch_shapes=[
            pltpu.VMEM((128, 128), F32),
            pltpu.VMEM((OWNERS * 8, 128), F32),
            pltpu.VMEM((176, 128), F32),
            pltpu.SemaphoreType.DMA((4,)),
            pltpu.VMEM((SAMPLES // STEPS, 128), BF16),
            pltpu.VMEM((SAMPLES, 128), BF16),
            pltpu.VMEM((3, rows_dev, SAMPLES), BF16),
            pltpu.SemaphoreType.DMA((FIELDS + 4,)),
        ],
        compiler_params=PART,
        cost_estimate=cost(1 << 30, 1 << 22),
    )(
        adjoint_state,
        lame_lambda,
        shear_modulus,
        buoyancy,
        in_hbm(receiver_cells.reshape(1, 4)),
        in_hbm(jnp.transpose(residual, (1, 0, 2))),
        in_hbm(sample_counts.reshape(1, rows_dev)),
        in_hbm(station_list.reshape(1, rows_dev)),
        in_hbm(jnp.asarray(resample_table())),
    )
    from_below = shift(up, 0, 1)
    from_above = shift(down, 0, -1)

    sources = lax.all_to_all(send, ("gx", "gy"), 0, 0, tiled=True)

    velocity, stress, mats, right, left = pl.pallas_call(
        edges_kernel,
        out_shape=held + (shape(EDGES + 1, 8, 128), shape(EDGES + 1, 8, 128)),
        in_specs=[VMEM] * 6,
        out_specs=(VMEM,) * 5,
        input_output_aliases={0: 0, 1: 1, 2: 2},
        compiler_params=PART,
        cost_estimate=cost(1 << 20, 1 << 21),
    )(velocity, stress, mats, from_below, from_above, up)
    from_left = shift(right, 1, 0)
    from_right = shift(left, -1, 0)

    velocity, stress, send, strip_v = pl.pallas_call(
        step_kernel,
        out_shape=held[:2] + (pltpu.HBM((256, 128), F32), pltpu.HBM((6, ROWS, 128), F32)),
        in_specs=[VMEM] * 7 + [ANY] * 2 + [VMEM] * 2,
        out_specs=(VMEM, VMEM, ANY, ANY),
        input_output_aliases={0: 0, 1: 1},
        scratch_shapes=[
            pltpu.VMEM((6, ROWS, 128), F32),
            pltpu.VMEM((12, ROWS, 128), F32),
            pltpu.VMEM((6, ROWS, 128), F32),
            pltpu.VMEM((STEPS, NZ, CY, CX), BF16),
            pltpu.VMEM((STEPS, NZ, CY, CX), BF16),
            pltpu.VMEM((24 * ROWS, 256), F32),
            pltpu.VMEM((2 * NZ * CY, 128), F32),
            pltpu.VMEM((256, 128), F32),
            pltpu.SemaphoreType.DMA((2 * STEPS + 1,)),
        ],
        compiler_params=PART,
        cost_estimate=cost(1 << 27, 1 << 23),
    )(
        velocity,
        stress,
        mats,
        right,
        left,
        from_left,
        from_right,
        forward_dilation,
        forward_shear,
        sources,
        in_hbm(tile_map.reshape(1, 256)),
    )
    got = lax.all_to_all(send, ("gx", "gy"), 0, 0, tiled=True)
    _, adjoint_out = pl.pallas_call(
        finish_kernel,
        out_shape=(held[1], shape(WAVES, NZ, CY, CX)),
        in_specs=[VMEM] * 3 + [ANY],
        out_specs=(VMEM, ANY),
        input_output_aliases={1: 0},
        scratch_shapes=[pltpu.VMEM((6, ROWS, 128), F32), pltpu.SemaphoreType.DMA((27,))],
        compiler_params=PART,
        cost_estimate=cost(1 << 24, 1 << 22),
    )(velocity, stress, mats, strip_v)
    kernels = pl.pallas_call(
        turn_kernel,
        out_shape=shape(16, 256),
        in_specs=[VMEM],
        out_specs=VMEM,
        compiler_params=PART,
    )(got)
    return kernels.reshape(2, NZ, 256), adjoint_out


def solution(mesh):
    in_specs = (
        P(None, None, "gy", "gx"),
        P(None, "gy", "gx"),
        P(None, "gy", "gx"),
        P(None, "gy", "gx"),
        P(None, None, "gy", "gx"),
        P(None, None, "gy", "gx"),
        P(("gx", "gy"), None, None),
        P(("gx", "gy")),
        P(("gx", "gy")),
        P(("gx", "gy")),
        P(("gx", "gy")),
    )
    out_specs = (P(None, None, ("gx", "gy")), P(None, None, "gy", "gx"))
    return jax.shard_map(local, mesh=mesh, in_specs=in_specs, out_specs=out_specs, check_vma=False)
```
